128 devices in a mesh: ctx: 16 (over z, x), tp: 8 (over y, core).
Axes of the slice: x: 4, y: 4, z: 4, core: 2. Of those that a mesh axis runs over, the one named last changes fastest.
Arguments:
- activations: bfloat16 [8192, 6144], P(('ctx', 'tp')), may hold values from -6 to 6
- w_qkv: bfloat16 [3, 6144, 4096], P(None, None, 'tp'), may hold values from -0.078125 to 0.078125
- log_decay: float32 [8192, 32], P('ctx', 'tp'), may hold values from -0.6 to 0, as said below
- gain: float32 [4096], P('tp'), may hold values from 0.1 to 1.9
- w_out: bfloat16 [4096, 6144], P('tp', 'ctx'), may hold values from -0.09375 to 0.09375
Outputs:
- layer_out: bfloat16 [8192, 6144], P(('ctx', 'tp'))
The draws below stay inside these ranges and needn't reach their ends.
Inputs may be any that keep to these rules, and one draw needn't show every extreme that they name: `log_decay`: every entry is negative.
All inputs are finite; a program needn't handle non-finite values.
Results may differ from the reference program's by a relative error of at most 0.022.
Values may be sent and summed in bfloat16 or wider, within the bound.
No kernel may reach another device: no remote copies, remote signals or barrier semaphores. Data moves between devices by JAX's collectives and lax.ppermute only.
A program may use at most 128 MiB of HBM per device.

```python
import math
import jax
import jax.numpy as jnp
from jax import lax

D = 6144
HEAD_DIM = 128
HEADS = 32
TOK_DEV = 512
TOKENS = 8192
N_TP = 8


def draw_log_decay(key, part):
    key = jax.random.fold_in(key, 11)
    keys_all = jax.random.split(key, 6)
    share = 0.5
    slow_heads = jax.random.uniform(keys_all[0], (HEADS,)) < share
    slow_rate = jnp.exp(jax.random.uniform(keys_all[1], (HEADS,), jnp.float32, math.log(0.05), 0.0)) / TOKENS
    fast_rate = jnp.exp(jax.random.uniform(keys_all[2], (HEADS,), jnp.float32, math.log(1.0 / 50.0), math.log(1.0 / 30.0)))
    rate = jnp.where(slow_heads, slow_rate, fast_rate)
    jitter = jax.random.uniform(keys_all[3], (TOKENS, HEADS), jnp.float32, 0.5, 1.5)
    decay = -rate[None, :] * jitter
    places = jax.random.randint(keys_all[4], (2, HEADS), 0, TOKENS)
    kept = jax.random.uniform(keys_all[5], (2, HEADS), jnp.float32, 0.6, 0.85)
    columns = jnp.broadcast_to(jnp.arange(HEADS)[None, :], (2, HEADS))
    decay = decay.at[places, columns].add(jnp.log(kept))
    return decay.astype(jnp.float32)


def block_scale(key, shape, shards, least, high):
    level = 1.0
    for axis_at, parts in shards:
        steps = jax.random.uniform(jax.random.fold_in(jax.random.fold_in(key, 6), axis_at), (parts,), jnp.float32, least / len(shards), high / len(shards))
        level = level * jnp.repeat(jnp.exp(steps), shape[axis_at] // parts).reshape((-1,) + (1,) * (len(shape) - 1 - axis_at))
    return level


def scatter_about(own_key, extent, scale, most, cuts=(), dtype=jnp.bfloat16):
    result = jax.random.normal(own_key, extent, jnp.float32) * scale
    if len(cuts) > 0:
        result = block_scale(own_key, extent, cuts, -0.22, 0.18) * result
    return jnp.clip(result, min=-most, max=most).astype(dtype)


def setup_inputs(seed: int = 0) -> dict:
    arg_keys = jax.random.split(jax.random.key(seed), 6)
    activations = scatter_about(arg_keys[0], (TOKENS, D), 1.0, 6.0, ((0, 128),))
    w_qkv = scatter_about(arg_keys[1], (3, D, HEADS * HEAD_DIM), D ** -0.5, 0.078125, ((2, 8),))
    log_decay = draw_log_decay(jax.random.fold_in(arg_keys[5], 71), 0)
    gain = jnp.clip(1.0 + 0.18 * jax.random.normal(arg_keys[3], (HEADS * HEAD_DIM,), jnp.float32), 0.1, 1.9)
    w_out = scatter_about(arg_keys[4], (HEADS * HEAD_DIM, D), (HEADS * HEAD_DIM) ** -0.5, 0.09375, ((0, 8), (1, 16)))
    return dict(activations=activations, w_qkv=w_qkv, log_decay=log_decay, gain=gain, w_out=w_out)


norm_eps = 1e-06

def reference(activations, w_qkv, log_decay, gain, w_out):
    projected = [jnp.dot(activations, w_qkv[member], preferred_element_type=jnp.float32) for member in range(3)]
    query = jax.nn.silu(projected[0]).astype(jnp.bfloat16)
    keys = jax.nn.silu(projected[1]).astype(jnp.bfloat16)
    values = projected[2].astype(jnp.bfloat16)
    block_count = TOKENS // TOK_DEV
    shaped = (block_count, TOK_DEV, HEADS, HEAD_DIM)
    inputs = (query.reshape(shaped), keys.reshape(shaped), values.reshape(shaped), log_decay.reshape(block_count, TOK_DEV, HEADS))
    lower = jnp.arange(TOK_DEV)[:, None] >= jnp.arange(TOK_DEV)[None, :]

    def advance(carried, block):
        query_b, keys_b, values_b, decay_b = block
        cumul = jnp.cumsum(decay_b, axis=0)
        final = cumul[-1]
        scores = jnp.einsum('rhd,shd->hrs', query_b.astype(jnp.float32), keys_b.astype(jnp.float32), precision=lax.Precision.HIGHEST)
        lagged = cumul.T[:, :, None] - cumul.T[:, None, :]
        weight = jnp.where(lower[None], jnp.exp(jnp.minimum(lagged, 0.0)), 0.0)
        probs = (scores * weight).astype(jnp.bfloat16)
        inner = jnp.einsum('hrs,shd->rhd', probs.astype(jnp.float32), values_b.astype(jnp.float32), precision=lax.Precision.HIGHEST)
        scaled_q = query_b.astype(jnp.float32) * jnp.exp(cumul)[:, :, None]
        outer = jnp.einsum('rhd,hde->rhe', scaled_q, carried, precision=lax.Precision.HIGHEST)
        scaled_k = keys_b.astype(jnp.float32) * jnp.exp(final[None, :] - cumul)[:, :, None]
        local_state = jnp.einsum('shd,she->hde', scaled_k, values_b.astype(jnp.float32), precision=lax.Precision.HIGHEST)
        updated = jnp.exp(final)[:, None, None] * carried + local_state
        return (updated, inner + outer)
    start_state = jnp.zeros((HEADS, HEAD_DIM, HEAD_DIM), jnp.float32)
    _, mixed = lax.scan(advance, start_state, inputs)
    mixed = mixed.reshape(TOKENS, HEADS, HEAD_DIM)
    scale = lax.rsqrt(lax.optimization_barrier(jnp.mean(mixed * mixed, axis=-1, keepdims=True)) + norm_eps)
    normed = (mixed * scale * gain.reshape(HEADS, HEAD_DIM)).astype(jnp.bfloat16).reshape(TOKENS, HEADS * HEAD_DIM)
    group_width = HEADS * HEAD_DIM // N_TP
    total = jnp.zeros((TOKENS, D), jnp.float32)
    for member in range(N_TP):
        lo_col = member * group_width
        part_out = jnp.dot(normed[:, lo_col:lo_col + group_width], w_out[lo_col:lo_col + group_width], preferred_element_type=jnp.float32).astype(jnp.bfloat16)
        total = total + lax.optimization_barrier(part_out).astype(jnp.float32)
    return total.astype(jnp.bfloat16)
```

```python
import jax
import jax.numpy as jnp
from jax import lax
from jax.sharding import PartitionSpec as P

norm_eps = 1e-06


def body(activations, w_qkv, log_decay, gain, w_out):
    heads = log_decay.shape[1]
    size = w_qkv.shape[2] // heads
    place = lax.axis_index("ctx")
    n_ctx = lax.axis_size("ctx")
    x = lax.all_gather(activations, "tp", axis=0, tiled=True)
    w_all = lax.all_gather(w_out, "ctx", axis=0)
    rows = x.shape[0]
    cumul = jnp.cumsum(log_decay.T, axis=1)
    final = cumul[:, -1]
    finals = lax.all_gather(final, "ctx")

    def split(a):
        return a.reshape(rows, heads, size)

    keys = split(jax.nn.silu(jnp.dot(x, w_qkv[1], preferred_element_type=jnp.float32)).astype(jnp.bfloat16))
    values = split(jnp.dot(x, w_qkv[2], preferred_element_type=jnp.float32).astype(jnp.bfloat16))
    scaled_k = (keys.astype(jnp.float32) * jnp.exp(final[:, None] - cumul).T[:, :, None]).astype(jnp.bfloat16)
    local_state = jnp.einsum("shd,she->hde", scaled_k, values, preferred_element_type=jnp.float32)
    states = lax.all_gather(local_state.astype(jnp.bfloat16), "ctx")
    block = jnp.arange(n_ctx)
    between = (block[None, :] > block[:, None]) & (block[None, :] < place)
    span = jnp.sum(jnp.where(between[:, :, None], finals[None], 0.0), axis=1)
    reach = jnp.where((block < place)[:, None], jnp.exp(span), 0.0)
    query = split(jax.nn.silu(jnp.dot(x, w_qkv[0], preferred_element_type=jnp.float32)).astype(jnp.bfloat16))
    scores = jnp.einsum("rhd,shd->hrs", query, keys, preferred_element_type=jnp.float32)
    lower = jnp.arange(rows)[:, None] >= jnp.arange(rows)[None, :]
    lagged = cumul[:, :, None] - cumul[:, None, :]
    weight = jnp.where(lower[None], jnp.exp(jnp.minimum(lagged, 0.0)), 0.0)
    probs = (scores * weight).astype(jnp.bfloat16)
    inner = jnp.einsum("hrs,shd->hrd", probs, values, preferred_element_type=jnp.float32)
    scaled_q = (query.astype(jnp.float32) * jnp.exp(cumul).T[:, :, None]).astype(jnp.bfloat16)
    carried = jnp.sum(states.astype(jnp.float32) * reach[:, :, None, None], axis=0)
    outer = jnp.einsum("rhd,hde->hre", scaled_q, carried.astype(jnp.bfloat16), preferred_element_type=jnp.float32)
    mixed = inner + outer
    scale = lax.rsqrt(jnp.mean(mixed * mixed, axis=-1, keepdims=True) + norm_eps)
    normed = (mixed * scale * gain.reshape(heads, 1, size)).astype(jnp.bfloat16)
    normed = normed.transpose(1, 0, 2).reshape(rows, heads * size)
    parts = jnp.einsum("rh,chd->rcd", normed, w_all, preferred_element_type=jnp.float32).astype(jnp.bfloat16)
    parts = parts.reshape(rows, -1)
    return lax.psum_scatter(parts, "tp", scatter_dimension=0, tiled=True)


def solution(mesh):
    in_specs = (
        P(("ctx", "tp"), None),
        P(None, None, "tp"),
        P("ctx", "tp"),
        P("tp"),
        P("tp", "ctx"),
    )
    out_specs = P(("ctx", "tp"), None)
    return jax.shard_map(body, mesh=mesh, in_specs=in_specs, out_specs=out_specs, check_vma=False)
```

```python
import functools

import jax
import jax.numpy as jnp
from jax import lax
from jax.experimental import pallas as pl
from jax.experimental.pallas import tpu as pltpu
from jax.sharding import PartitionSpec as P

norm_eps = 1e-06
f32, bf16 = jnp.float32, jnp.bfloat16
HEADS, SIZE = 4, 128
WIDE = HEADS * SIZE
N_X = N_Z = N_Y = 4
VMEM_LIMIT = 40 * 2**20


def params(**kw):
    return pltpu.CompilerParams(vmem_limit_bytes=VMEM_LIMIT, **kw)


def cost(flops, nbytes):
    return pl.CostEstimate(flops=flops, bytes_accessed=nbytes, transcendentals=0)


def to_y(a, k):
    return lax.ppermute(a, "tp", [(i, (i // 2 + k) % N_Y * 2 + i % 2) for i in range(2 * N_Y)])


def to_sibling(a):
    return lax.ppermute(a, "tp", [(i, i ^ 1) for i in range(2 * N_Y)])


def to_x(a, k):
    return lax.ppermute(a, "ctx", [(j, j // N_X * N_X + (j + k) % N_X) for j in range(N_X * N_Z)])


def to_z(a, k):
    return lax.ppermute(a, "ctx", [(j, j + N_X * k) for j in range(N_X * N_Z) if j // N_X + k < N_Z])


def qkv_kernel(layout, *refs):
    pieces, w, out, rows = refs[: len(layout)], refs[len(layout)], refs[-2], refs[-1]
    step = pl.program_id(0)

    @pl.when(step == 0)
    def _():
        for piece, (row, col) in zip(pieces, layout):
            rows[row : row + piece.shape[0], col : col + piece.shape[1]] = piece[...]

    acc = jnp.dot(rows[...], w[0], preferred_element_type=f32)
    gated = acc / (1.0 + jnp.exp(-acc))
    out[...] = jnp.where(step < 4, gated, acc).astype(bf16)


def qkv(pieces, layout, count, w_qkv, block, held=None):
    depth = w_qkv.shape[1]
    tile = 256
    per = WIDE // tile
    kept = () if held is None else (held,)
    return pl.pallas_call(
        functools.partial(qkv_kernel, layout),
        grid=(3 * per,),
        out_shape=jax.ShapeDtypeStruct((512, 3 * WIDE), bf16),
        in_specs=[pl.BlockSpec(p.shape, lambda j: (0, 0)) for p in pieces]
        + [pl.BlockSpec((1, depth, tile), lambda j: (j // per, 0, j % per))]
        + [pl.BlockSpec(memory_space=pl.ANY)] * len(kept),
        out_specs=pl.BlockSpec((count, tile), lambda j: (block, j)),
        input_output_aliases={len(pieces) + 1: 0} if kept else {},
        scratch_shapes=[pltpu.VMEM((count, depth), bf16)],
        compiler_params=params(),
        cost_estimate=cost(2 * count * depth * 3 * WIDE, 3 * WIDE * depth * 2),
        name="qkv",
    )(*pieces, w_qkv, *kept)


def pack(out, last):
    high = last.astype(bf16).astype(f32)
    mid = (last - high).astype(bf16).astype(f32)
    low = last - high - mid
    out[WIDE:, :] = jnp.concatenate([high, mid, low, jnp.zeros_like(low)], axis=0).astype(bf16)


def unpack(ref):
    tail = ref[WIDE:, :].astype(f32)
    return tail[0:4] + tail[4:8] + tail[8:12]


def state_kernel(rows, g, last, out):
    for h in range(HEADS):
        keys = rows[:, WIDE + h * SIZE : WIDE + (h + 1) * SIZE].astype(f32)
        values = rows[:, 2 * WIDE + h * SIZE : 2 * WIDE + (h + 1) * SIZE]
        scaled = (keys * jnp.exp(last[h : h + 1, 0:1] - g[:, h : h + 1])).astype(bf16)
        state = lax.dot_general(scaled, values, (((0,), (0,)), ((), ())), preferred_element_type=f32)
        out[h * SIZE : (h + 1) * SIZE, :] = state.astype(bf16)
    pack(out, last[...])


def inner_kernel(at, rows, g, gt, out):
    def position(idx):
        chunk = idx >> 7
        ahead = jnp.where(chunk == 0, 1, jnp.where(chunk == 1, 3, jnp.where(chunk == 2, 0, 2)))
        return ((at[0] + ahead) & 3) * 128 + ((at[1] + (idx >> 6)) & 1) * 64 + (idx & 63)

    n = g.shape[0]
    row = position(lax.broadcasted_iota(jnp.int32, (n, 1), 0))
    col = position(lax.broadcasted_iota(jnp.int32, (1, n), 1))
    lower = row >= col
    for h in range(HEADS):
        query = rows[:, h * SIZE : (h + 1) * SIZE]
        keys = rows[:, WIDE + h * SIZE : WIDE + (h + 1) * SIZE]
        values = rows[:, 2 * WIDE + h * SIZE : 2 * WIDE + (h + 1) * SIZE]
        scores = lax.dot_general(query, keys, (((1,), (1,)), ((), ())), preferred_element_type=f32)
        lagged = g[:, h : h + 1] - gt[h : h + 1, :]
        probs = jnp.where(lower, scores * jnp.exp(jnp.minimum(lagged, 0.0)), 0.0).astype(bf16)
        out[:, h * SIZE : (h + 1) * SIZE] = jnp.dot(probs, values, preferred_element_type=f32)


def row_kernel(at, s0, s1, s2, s3, before, total):
    refs = (s0, s1, s2, s3)
    x = at[2]
    place = [(x - k) & 3 for k in range(N_X)]
    last = [unpack(ref) for ref in refs]

    def between(k, end):
        return sum(jnp.where((place[m] > place[k]) & (place[m] < end), last[m], 0.0) for m in range(N_X))

    reach = [jnp.where(place[k] < x, jnp.exp(between(k, x)), 0.0) for k in range(N_X)]
    whole = [jnp.exp(between(k, N_X)) for k in range(N_X)]
    for h in range(HEADS):
        rows = slice(h * SIZE, (h + 1) * SIZE)
        states = [ref[rows, :].astype(f32) for ref in refs]
        before[rows, :] = sum(states[k] * reach[k][h : h + 1] for k in range(1, N_X))
        total[rows, :] = sum(states[k] * whole[k][h : h + 1] for k in range(N_X)).astype(bf16)
    pack(total, last[0] + last[1] + last[2] + last[3])
    lead = sum(jnp.where(place[k] < x, last[k], 0.0) for k in range(1, N_X))
    before[WIDE:, :] = jnp.concatenate([lead, lead], axis=0)


def normed_kernel(before, t1, t2, t3, qkv, g, inner, gain, out):
    lead = jnp.exp(before[WIDE : WIDE + HEADS, :])
    r1, r2 = unpack(t1), unpack(t2)
    reach2, reach3 = jnp.exp(r1), jnp.exp(r1 + r2)
    for h in range(HEADS):
        rows = slice(h * SIZE, (h + 1) * SIZE)
        one = slice(h, h + 1)
        earlier = (
            t1[rows, :].astype(f32) + t2[rows, :].astype(f32) * reach2[one] + t3[rows, :].astype(f32) * reach3[one]
        )
        carried = (earlier * lead[one] + before[rows, :]).astype(bf16)
        query = qkv[:, rows].astype(f32)
        scaled = (query * jnp.exp(g[:, one])).astype(bf16)
        mixed = inner[:, rows] + jnp.dot(scaled, carried, preferred_element_type=f32)
        scale = lax.rsqrt(jnp.mean(mixed * mixed, axis=-1, keepdims=True) + norm_eps)
        out[:, rows] = (mixed * scale * gain[:, rows]).astype(bf16)


def whole_call(kernel, args, outs, name, flops, scalars=0):
    nbytes = sum(a.size * a.dtype.itemsize for a in args)
    return pl.pallas_call(
        kernel,
        out_shape=outs,
        in_specs=[pl.BlockSpec(memory_space=pltpu.SMEM)] * scalars
        + [pl.BlockSpec(memory_space=pltpu.VMEM)] * (len(args) - scalars),
        out_specs=jax.tree.map(lambda _: pl.BlockSpec(memory_space=pltpu.VMEM), outs),
        compiler_params=params(),
        cost_estimate=cost(flops, nbytes),
        name=name,
    )(*args)


def project_kernel(n, per, *refs):
    chunks, w, outs = refs[:n], refs[n], refs[n + 1 :]
    rows = jnp.concatenate([chunk[...] for chunk in chunks], axis=0)
    width = w.shape[2]
    for m in range(per):
        part = jnp.dot(rows, w[m], preferred_element_type=f32).astype(bf16)
        for i, out in enumerate(outs):
            out[:, m * width : (m + 1) * width] = part[i * 64 : (i + 1) * 64]


def project(normed, w_all, places):
    n_ctx, depth, width = w_all.shape
    per = 4
    half = jax.ShapeDtypeStruct((64, n_ctx * width), bf16)
    n = len(places)
    return pl.pallas_call(
        functools.partial(project_kernel, n, per),
        grid=(n_ctx // per,),
        out_shape=[half] * (2 * n),
        in_specs=[pl.BlockSpec((128, depth), lambda j, r=r: (r, 0)) for r in places]
        + [pl.BlockSpec((per, depth, width), lambda j: (j, 0, 0))],
        out_specs=[pl.BlockSpec((64, per * width), lambda j: (0, j))] * (2 * n),
        compiler_params=params(),
        cost_estimate=cost(2 * n * 128 * depth * n_ctx * width, 2 * depth * n_ctx * width),
        name="project",
    )(*[normed] * n, w_all)


def plus(*terms):
    total = terms[0].astype(f32)
    for term in terms[1:]:
        total = total + term.astype(f32)
    return total.astype(bf16)


def body(activations, w_qkv, log_decay, gain, w_out):
    tp, ctx = lax.axis_index("tp"), lax.axis_index("ctx")
    y, core = tp // 2, tp % 2
    at = jnp.stack([y, core, ctx % N_X]).astype(jnp.int32)
    w_all = lax.all_gather(w_out, "ctx", axis=0)

    cumul = jnp.cumsum(log_decay.T, axis=1)
    last = jnp.broadcast_to(cumul[:, -1:], (HEADS, SIZE))
    gt = jnp.roll(cumul.reshape(HEADS, N_Y, 2, 64), -y, axis=1)
    gt = jnp.where(core == 0, gt, gt[:, :, ::-1])
    gt = jnp.stack([gt[:, 1], gt[:, 3], gt[:, 0], gt[:, 2]], axis=1).reshape(HEADS, 512)
    g = gt.T

    mid = activations.shape[1] // 2
    left, right = to_y(activations, 1), to_y(activations, -1)
    own2 = to_sibling(activations)
    rows = qkv([activations, own2], [(0, 0), (64, 0)], 128, w_qkv, 2)
    left, right, rows = lax.optimization_barrier((left, right, rows))
    far_l, far_r = to_y(left[:, :mid], 1), to_y(right[:, mid:], -1)
    left2, right2 = to_sibling(left), to_sibling(right)
    rows = qkv([right, right2, left, left2], [(0, 0), (64, 0), (128, 0), (192, 0)], 256, w_qkv, 0, rows)
    far_l, far_r, rows = lax.optimization_barrier((far_l, far_r, rows))
    far_l2, far_r2 = to_sibling(far_l), to_sibling(far_r)
    rows = qkv([far_l, far_r, far_l2, far_r2], [(0, 0), (0, mid), (64, 0), (64, mid)], 128, w_qkv, 3, rows)

    packed = jax.ShapeDtypeStruct((WIDE + 16, SIZE), bf16)
    state = whole_call(state_kernel, (rows, g, last), packed, "state", 2 * 512 * WIDE * SIZE)
    row = [state] + [to_x(state, k) for k in range(1, N_X)]
    inner = whole_call(
        inner_kernel, (at, rows, g, gt), jax.ShapeDtypeStruct((512, WIDE), f32), "inner", 4 * 512 * 512 * WIDE, 1
    )
    before, total = whole_call(
        row_kernel, (at, *row), (jax.ShapeDtypeStruct((WIDE + 8, SIZE), f32), packed), "row", 10 * WIDE * SIZE, 1
    )
    totals = [to_z(total, k) for k in range(1, N_Z)]
    normed = whole_call(
        normed_kernel,
        (before, *totals, rows, g, inner, gain.reshape(1, WIDE)),
        jax.ShapeDtypeStruct((512, WIDE), bf16),
        "normed",
        2 * 512 * WIDE * SIZE,
    )

    far_own, far_sib = project(normed, w_all, (3,))
    far = plus(far_own, to_sibling(far_sib))
    from_l, from_r = to_y(far[:, :mid], 1), to_y(far[:, mid:], -1)
    up_own, up_sib, down_own, down_sib = project(normed, w_all, (0, 1))
    up, down = plus(up_own, to_sibling(up_sib)), plus(down_own, to_sibling(down_sib))
    up_plain, down_plain = to_y(up[:, mid:], 1), to_y(down[:, :mid], -1)
    up_sum, down_sum = to_y(plus(up[:, :mid], from_l), 1), to_y(plus(down[:, mid:], from_r), -1)
    normed, up, down = lax.optimization_barrier((normed, up, down))
    here_own, here_sib = project(normed, w_all, (2,))
    here_sib = to_sibling(here_sib)
    first = plus(here_own[:, :mid], here_sib[:, :mid], down_plain, up_sum)
    second = plus(here_own[:, mid:], here_sib[:, mid:], up_plain, down_sum)
    return jnp.concatenate([first, second], axis=1)


def solution(mesh):
    in_specs = (
        P(("ctx", "tp"), None),
        P(None, None, "tp"),
        P("ctx", "tp"),
        P("tp"),
        P("tp", "ctx"),
    )
    out_specs = P(("ctx", "tp"), None)
    return jax.shard_map(body, mesh=mesh, in_specs=in_specs, out_specs=out_specs, check_vma=False)
```

```python
import functools

import jax
import jax.numpy as jnp
import numpy as np
from jax import lax
from jax.experimental import pallas as pl
from jax.experimental.pallas import tpu as pltpu
from jax.sharding import PartitionSpec as P

norm_eps = 1e-06
f32, bf16 = jnp.float32, jnp.bfloat16
HEADS, SIZE = 4, 128
WIDE = HEADS * SIZE
N_X = N_Z = N_Y = 4
PLACES = ((1, 0), (3, 0), (0, 0), (0, 1), (1, 1), (3, 1), (2, 0), (2, 1))
SHARE = 0.01
VMEM_LIMIT = 20 * 2**20


def params(**kw):
    return pltpu.CompilerParams(vmem_limit_bytes=VMEM_LIMIT, **kw)


def cost(flops, nbytes):
    return pl.CostEstimate(flops=int(flops * SHARE), bytes_accessed=int(nbytes * SHARE), transcendentals=0)


def to_y(a, k):
    return lax.ppermute(a, "tp", [(i, (i // 2 + k) % N_Y * 2 + i % 2) for i in range(2 * N_Y)])


def to_sibling(a):
    return lax.ppermute(a, "tp", [(i, i ^ 1) for i in range(2 * N_Y)])


def to_x(a, k):
    return lax.ppermute(a, "ctx", [(j, j // N_X * N_X + (j + k) % N_X) for j in range(N_X * N_Z)])


def to_z(a, k):
    return lax.ppermute(a, "ctx", [(j, j + N_X * k) for j in range(N_X * N_Z) if j // N_X + k < N_Z])


def place_rows(pieces, layout, rows):
    for piece, (row, col) in zip(pieces, layout):
        rows[row : row + piece.shape[0], col : col + piece.shape[1]] = piece[...]


def activate(member, acc):
    return (acc if member == 2 else acc / (1.0 + jnp.exp(-acc))).astype(bf16)


def qkv_first_kernel(layout, *refs):
    n = len(layout)
    pieces, w, out, held, rows, sems = refs[:n], refs[n], *refs[n + 1 :]
    depth = w.shape[1]
    cut = depth // 4
    copies = [
        [
            pltpu.make_async_copy(w.at[m, pl.ds(k * cut, cut)], held.at[m, pl.ds(k * cut, cut)], sems.at[m, k])
            for k in range(4)
        ]
        for m in range(3)
    ]
    for m in range(3):
        for k in range(4):
            copies[m][k].start()
    place_rows(pieces, layout, rows)
    for m in range(3):
        acc = None
        for k in range(4):
            copies[m][k].wait()
            part = jnp.dot(
                rows[:, k * cut : (k + 1) * cut], held[m, k * cut : (k + 1) * cut], preferred_element_type=f32
            )
            acc = part if acc is None else acc + part
        out[:, m * WIDE : (m + 1) * WIDE] = activate(m, acc)


def qkv_kernel(layout, *refs):
    n = len(layout)
    pieces, w, out, rows = refs[:n], refs[n], refs[n + 1], refs[n + 2]
    place_rows(pieces, layout, rows)
    tile = 256
    for m in range(3):
        for start in range(0, WIDE, tile):
            acc = jnp.dot(rows[...], w[m, :, start : start + tile], preferred_element_type=f32)
            out[:, m * WIDE + start : m * WIDE + start + tile] = activate(m, acc)


def qkv(pieces, layout, count, w, first=False):
    depth = w.shape[1]
    out = jax.ShapeDtypeStruct((count, 3 * WIDE), bf16)
    vmem = pl.BlockSpec(memory_space=pltpu.VMEM)
    return pl.pallas_call(
        functools.partial(qkv_first_kernel if first else qkv_kernel, layout),
        out_shape=(out, pltpu.VMEM(w.shape, bf16)) if first else out,
        in_specs=[vmem] * len(pieces) + [pl.BlockSpec(memory_space=pltpu.HBM) if first else vmem],
        out_specs=(vmem, vmem) if first else vmem,
        scratch_shapes=[pltpu.VMEM((count, depth), bf16)] + ([pltpu.SemaphoreType.DMA((3, 4))] if first else []),
        compiler_params=params(),
        cost_estimate=cost(2 * count * depth * 3 * WIDE, 3 * WIDE * depth * 2),
        name="qkv",
    )(*pieces, w)


def columns(refs, start):
    return jnp.concatenate([ref[:, start : start + SIZE] for ref in refs], axis=0)


def pack(out, last):
    high = last.astype(bf16).astype(f32)
    mid = (last - high).astype(bf16).astype(f32)
    low = last - high - mid
    out[WIDE:, :] = jnp.concatenate([high, mid, low, jnp.zeros_like(low)], axis=0).astype(bf16)


def unpack(ref):
    tail = ref[WIDE:, :].astype(f32)
    return tail[0:4] + tail[4:8] + tail[8:12]


def state_kernel(a, b, c, g, last, out):
    for h in range(HEADS):
        keys = columns((a, b, c), WIDE + h * SIZE).astype(f32)
        values = columns((a, b, c), 2 * WIDE + h * SIZE)
        scaled = (keys * jnp.exp(last[h : h + 1, 0:1] - g[:, h : h + 1])).astype(bf16)
        state = lax.dot_general(scaled, values, (((0,), (0,)), ((), ())), preferred_element_type=f32)
        out[h * SIZE : (h + 1) * SIZE, :] = state.astype(bf16)
    pack(out, last[...])


def inner_kernel(a, b, c, g, gt, row, col, out):
    lower = row[...] >= col[...]
    for h in range(HEADS):
        query = columns((a, b, c), h * SIZE)
        keys = columns((a, b, c), WIDE + h * SIZE)
        values = columns((a, b, c), 2 * WIDE + h * SIZE)
        scores = lax.dot_general(query, keys, (((1,), (1,)), ((), ())), preferred_element_type=f32)
        lagged = g[:, h : h + 1] - gt[h : h + 1, :]
        probs = jnp.where(lower, scores * jnp.exp(jnp.minimum(lagged, 0.0)), 0.0).astype(bf16)
        out[:, h * SIZE : (h + 1) * SIZE] = jnp.dot(probs, values, preferred_element_type=f32)


def row_kernel(at, s0, s1, s2, s3, before, total):
    refs = (s0, s1, s2, s3)
    x = at[0]
    place = [(x - k) & 3 for k in range(N_X)]
    last = [unpack(ref) for ref in refs]

    def between(k, end):
        return sum(jnp.where((place[m] > place[k]) & (place[m] < end), last[m], 0.0) for m in range(N_X))

    reach = [jnp.where(place[k] < x, jnp.exp(between(k, x)), 0.0) for k in range(N_X)]
    whole = [jnp.exp(between(k, N_X)) for k in range(N_X)]
    for h in range(HEADS):
        rows = slice(h * SIZE, (h + 1) * SIZE)
        states = [ref[rows, :].astype(f32) for ref in refs]
        before[rows, :] = sum(states[k] * reach[k][h : h + 1] for k in range(1, N_X))
        total[rows, :] = sum(states[k] * whole[k][h : h + 1] for k in range(N_X)).astype(bf16)
    pack(total, last[0] + last[1] + last[2] + last[3])
    lead = sum(jnp.where(place[k] < x, last[k], 0.0) for k in range(1, N_X))
    before[WIDE:, :] = jnp.concatenate([lead, lead], axis=0)


def normed_kernel(before, t1, t2, t3, a, b, c, g, inner, gain, out):
    lead = jnp.exp(before[WIDE : WIDE + HEADS, :])
    r1, r2 = unpack(t1), unpack(t2)
    reach2, reach3 = jnp.exp(r1), jnp.exp(r1 + r2)
    for h in range(HEADS):
        rows = slice(h * SIZE, (h + 1) * SIZE)
        one = slice(h, h + 1)
        earlier = (
            t1[rows, :].astype(f32) + t2[rows, :].astype(f32) * reach2[one] + t3[rows, :].astype(f32) * reach3[one]
        )
        carried = (earlier * lead[one] + before[rows, :]).astype(bf16)
        query = columns((a, b, c), h * SIZE).astype(f32)
        scaled = (query * jnp.exp(g[:, one])).astype(bf16)
        mixed = inner[:, rows] + jnp.dot(scaled, carried, preferred_element_type=f32)
        scale = lax.rsqrt(jnp.mean(mixed * mixed, axis=-1, keepdims=True) + norm_eps)
        out[:, rows] = (mixed * scale * gain[:, rows]).astype(bf16)


def whole_call(kernel, args, outs, name, flops, scalars=0):
    nbytes = sum(a.size * a.dtype.itemsize for a in args)
    return pl.pallas_call(
        kernel,
        out_shape=outs,
        in_specs=[pl.BlockSpec(memory_space=pltpu.SMEM)] * scalars
        + [pl.BlockSpec(memory_space=pltpu.VMEM)] * (len(args) - scalars),
        out_specs=jax.tree.map(lambda _: pl.BlockSpec(memory_space=pltpu.VMEM), outs),
        compiler_params=params(),
        cost_estimate=cost(flops, nbytes),
        name=name,
    )(*args)


def project_part(rows, w, outs, m):
    width = w.shape[2]
    part = jnp.dot(rows, w[m], preferred_element_type=f32).astype(bf16)
    for i, out in enumerate(outs):
        out[:, m * width : (m + 1) * width] = part[i * 64 : (i + 1) * 64]


def project_first_kernel(start, normed, w, own, sib, held, sems):
    per = w.shape[0] // 4
    copies = [
        pltpu.make_async_copy(w.at[pl.ds(i * per, per)], held.at[pl.ds(i * per, per)], sems.at[i]) for i in range(4)
    ]
    for copy in copies:
        copy.start()
    rows = normed[start : start + 128, :]
    for i in range(4):
        copies[i].wait()
        for m in range(i * per, (i + 1) * per):
            project_part(rows, held, (own, sib), m)


def project_kernel(blocks, normed, w, *outs):
    rows = jnp.concatenate([normed[64 * b : 64 * b + 64, :] for b in blocks], axis=0)
    for m in range(w.shape[0]):
        project_part(rows, w, outs, m)


def project(normed, w, blocks, first=False):
    n_ctx, depth, width = w.shape
    vmem = pl.BlockSpec(memory_space=pltpu.VMEM)
    n = len(blocks)
    count = 64 * n
    outs = [jax.ShapeDtypeStruct((64, n_ctx * width), bf16)] * n
    if first:
        kernel = functools.partial(project_first_kernel, blocks[0] * 64)
        outs = outs + [pltpu.VMEM(w.shape, bf16)]
    else:
        kernel = functools.partial(project_kernel, blocks)
    return pl.pallas_call(
        kernel,
        out_shape=outs,
        in_specs=[vmem, pl.BlockSpec(memory_space=pltpu.HBM) if first else vmem],
        out_specs=[vmem] * len(outs),
        scratch_shapes=[pltpu.SemaphoreType.DMA((4,))] if first else [],
        compiler_params=params(),
        cost_estimate=cost(2 * count * depth * n_ctx * width, 2 * depth * n_ctx * width),
        name="project",
    )(normed, w)


def final_kernel(own, sib, up_plain, down_plain, up_sum, down_sum, out):
    mid = up_sum.shape[1]
    for start, one, two in ((0, down_plain, up_sum), (mid, up_plain, down_sum)):
        at = slice(start, start + mid)
        total = own[:, at].astype(f32) + sib[:, at].astype(f32) + one[...].astype(f32) + two[...].astype(f32)
        out[:, at] = total.astype(bf16)


def after(value, *others):
    return lax.optimization_barrier((value, *others))[0]


def plus(*terms):
    total = terms[0].astype(f32)
    for term in terms[1:]:
        total = total + term.astype(f32)
    return total.astype(bf16)


def body(activations, w_qkv, log_decay, gain, w_out):
    tp, ctx = lax.axis_index("tp"), lax.axis_index("ctx")
    y, core = tp // 2, tp % 2
    at = (ctx % N_X).astype(jnp.int32).reshape(1)
    w_all = lax.all_gather(w_out, "ctx", axis=0)

    cumul = jnp.cumsum(log_decay.T, axis=1)
    last = jnp.broadcast_to(cumul[:, -1:], (HEADS, SIZE))
    gt = jnp.roll(cumul.reshape(HEADS, N_Y, 2, 64), -y, axis=1)
    gt = jnp.where(core == 0, gt, gt[:, :, ::-1])
    gt = jnp.concatenate([gt[:, chip, half] for chip, half in PLACES], axis=1)
    g = gt.T
    chip, half = (jnp.array(np.repeat(np.array(p), 64), jnp.int32) for p in zip(*PLACES))
    pos = ((chip + y) & 3) * 128 + ((half + core) & 1) * 64 + jnp.arange(512, dtype=jnp.int32) % 64

    depth = activations.shape[1]
    mid = depth // 2
    low, high = activations[:, :mid], activations[:, mid:]
    left_low, right_high = to_y(low, 1), to_y(high, -1)
    left_high, right_low = to_y(high, 1), to_y(low, -1)
    own2 = to_sibling(activations)
    own2 = after(own2, g, gt, last, at, pos)
    qkv_a, w_qkv = qkv([activations, own2], [(0, 0), (64, 0)], 128, w_qkv, True)
    left_low, right_high = after((left_low, right_high), qkv_a)
    far_low, far_high = to_y(left_low, 1), to_y(right_high, -1)
    low2, high2 = to_sibling(left_low), to_sibling(right_high)
    left_high2, right_low2 = to_sibling(left_high), to_sibling(right_low)
    near = [right_low, right_high, left_low, left_high]
    qkv_b = qkv(near, [(0, 0), (0, mid), (64, 0), (64, mid)], 128, w_qkv)
    far_low, far_high = after((far_low, far_high), qkv_b)
    rest = [right_low2, high2, low2, left_high2, far_low, far_high, to_sibling(far_low), to_sibling(far_high)]
    qkv_c = qkv(rest, [(64 * i, col) for i in range(4) for col in (0, mid)], 256, w_qkv)
    rows = (qkv_b, qkv_a, qkv_c)

    packed = jax.ShapeDtypeStruct((WIDE + 16, SIZE), bf16)
    state = whole_call(state_kernel, (*rows, g, last), packed, "state", 2 * 512 * WIDE * SIZE)
    row = [state] + [to_x(state, k) for k in range(1, N_X)]
    inner = whole_call(
        inner_kernel,
        (*rows, g, gt, pos.reshape(512, 1), pos.reshape(1, 512)),
        jax.ShapeDtypeStruct((512, WIDE), f32),
        "inner",
        4 * 512 * 512 * WIDE,
    )
    before, total = whole_call(
        row_kernel, (at, *row), (jax.ShapeDtypeStruct((WIDE + 8, SIZE), f32), packed), "row", 10 * WIDE * SIZE, 1
    )
    totals = [to_z(total, k) for k in range(1, N_Z)]
    normed = whole_call(
        normed_kernel,
        (before, *totals, *rows, g, inner, gain.reshape(1, WIDE)),
        jax.ShapeDtypeStruct((512, WIDE), bf16),
        "normed",
        2 * 512 * WIDE * SIZE,
    )

    w_all = pltpu.with_memory_space_constraint(w_all, pltpu.HBM)
    far_own, far_sib, w_all = project(normed, w_all, (6, 7), True)
    far_sib = to_sibling(far_sib)
    near_parts = project(normed, w_all, (0, 4, 1, 5))
    far_sib = after(far_sib, near_parts)
    up_own, up_sib, down_own, down_sib = near_parts
    from_l = to_y(plus(far_own[:, :mid], far_sib[:, :mid]), 1)
    from_r = to_y(plus(far_own[:, mid:], far_sib[:, mid:]), -1)
    up_sib, down_sib = to_sibling(up_sib), to_sibling(down_sib)
    up_plain = plus(up_own[:, mid:], up_sib[:, mid:])
    down_plain = plus(down_own[:, :mid], down_sib[:, :mid])
    normed = after(normed, up_plain, down_plain)
    up_plain, down_plain = to_y(up_plain, 1), to_y(down_plain, -1)
    here_own, here_sib = project(normed, w_all, (2, 3))
    from_l, from_r = after((from_l, from_r), here_own)
    up_sum = to_y(plus(up_own[:, :mid], up_sib[:, :mid], from_l), 1)
    down_sum = to_y(plus(down_own[:, mid:], down_sib[:, mid:], from_r), -1)
    here_sib = to_sibling(here_sib)
    return whole_call(
        final_kernel,
        (here_own, here_sib, up_plain, down_plain, up_sum, down_sum),
        jax.ShapeDtypeStruct((64, depth), bf16),
        "final",
        4 * 64 * depth,
    )


def solution(mesh):
    in_specs = (
        P(("ctx", "tp"), None),
        P(None, None, "tp"),
        P("ctx", "tp"),
        P("tp"),
        P("tp", "ctx"),
    )
    out_specs = P(("ctx", "tp"), None)
    return jax.shard_map(body, mesh=mesh, in_specs=in_specs, out_specs=out_specs, check_vma=False)
```

```python
import functools

import jax
import jax.numpy as jnp
import numpy as np
from jax import lax
from jax.experimental import pallas as pl
from jax.experimental.pallas import tpu as pltpu
from jax.sharding import PartitionSpec as P

norm_eps = 1e-06
f32, bf16 = jnp.float32, jnp.bfloat16
HEADS, SIZE = 4, 128
WIDE = HEADS * SIZE
N_X = N_Z = N_Y = 4
PLACES = ((1, 0), (3, 0), (0, 0), (0, 1), (1, 1), (3, 1), (2, 0), (2, 1))
SHARE = 0.01
VMEM_LIMIT = 20 * 2**20


def params(**kw):
    return pltpu.CompilerParams(vmem_limit_bytes=VMEM_LIMIT, **kw)


def cost(flops, nbytes):
    return pl.CostEstimate(flops=int(flops * SHARE), bytes_accessed=int(nbytes * SHARE), transcendentals=0)


def to_y(a, k):
    return lax.ppermute(a, "tp", [(i, (i // 2 + k) % N_Y * 2 + i % 2) for i in range(2 * N_Y)])


def to_sibling(a):
    return lax.ppermute(a, "tp", [(i, i ^ 1) for i in range(2 * N_Y)])


def to_x(a, k):
    return lax.ppermute(a, "ctx", [(j, j // N_X * N_X + (j + k) % N_X) for j in range(N_X * N_Z)])


def to_z(a, k):
    return lax.ppermute(a, "ctx", [(j, j + N_X * k) for j in range(N_X * N_Z) if j // N_X + k < N_Z])


def place_rows(pieces, layout, rows):
    for piece, (row, col) in zip(pieces, layout):
        rows[row : row + piece.shape[0], col : col + piece.shape[1]] = piece[...]


def activate(member, acc):
    return (acc if member == 2 else acc / (1.0 + jnp.exp(-acc))).astype(bf16)


def qkv_first_kernel(layout, *refs):
    n = len(layout)
    pieces, w, out, held, rows, sems = refs[:n], refs[n], *refs[n + 1 :]
    depth = w.shape[1]
    cut = depth // 4
    copies = [
        [
            pltpu.make_async_copy(w.at[m, pl.ds(k * cut, cut)], held.at[m, pl.ds(k * cut, cut)], sems.at[m, k])
            for k in range(4)
        ]
        for m in range(3)
    ]
    for m in range(3):
        for k in range(4):
            copies[m][k].start()
    place_rows(pieces, layout, rows)
    for m in range(3):
        acc = None
        for k in range(4):
            copies[m][k].wait()
            part = jnp.dot(
                rows[:, k * cut : (k + 1) * cut], held[m, k * cut : (k + 1) * cut], preferred_element_type=f32
            )
            acc = part if acc is None else acc + part
        out[:, m * WIDE : (m + 1) * WIDE] = activate(m, acc)


def qkv_kernel(layout, *refs):
    n = len(layout)
    pieces, w, out, rows = refs[:n], refs[n], refs[n + 1], refs[n + 2]
    place_rows(pieces, layout, rows)
    tile = 256
    for m in range(3):
        for start in range(0, WIDE, tile):
            acc = jnp.dot(rows[...], w[m, :, start : start + tile], preferred_element_type=f32)
            out[:, m * WIDE + start : m * WIDE + start + tile] = activate(m, acc)


def qkv(pieces, layout, count, w, first=False):
    depth = w.shape[1]
    out = jax.ShapeDtypeStruct((count, 3 * WIDE), bf16)
    vmem = pl.BlockSpec(memory_space=pltpu.VMEM)
    return pl.pallas_call(
        functools.partial(qkv_first_kernel if first else qkv_kernel, layout),
        out_shape=(out, pltpu.VMEM(w.shape, bf16)) if first else out,
        in_specs=[vmem] * len(pieces) + [pl.BlockSpec(memory_space=pltpu.HBM) if first else vmem],
        out_specs=(vmem, vmem) if first else vmem,
        scratch_shapes=[pltpu.VMEM((count, depth), bf16)] + ([pltpu.SemaphoreType.DMA((3, 4))] if first else []),
        compiler_params=params(),
        cost_estimate=cost(2 * count * depth * 3 * WIDE, 3 * WIDE * depth * 2),
        name="qkv",
    )(*pieces, w)


def columns(refs, start):
    return jnp.concatenate([ref[:, start : start + SIZE] for ref in refs], axis=0)


def pack(out, last):
    high = last.astype(bf16).astype(f32)
    mid = (last - high).astype(bf16).astype(f32)
    low = last - high - mid
    out[WIDE:, :] = jnp.concatenate([high, mid, low, jnp.zeros_like(low)], axis=0).astype(bf16)


def unpack(ref):
    tail = ref[WIDE:, :].astype(f32)
    return tail[0:4] + tail[4:8] + tail[8:12]


def state_kernel(a, b, c, g, last, out):
    for h in range(HEADS):
        keys = columns((a, b, c), WIDE + h * SIZE).astype(f32)
        values = columns((a, b, c), 2 * WIDE + h * SIZE)
        scaled = (keys * jnp.exp(last[h : h + 1, 0:1] - g[:, h : h + 1])).astype(bf16)
        state = lax.dot_general(scaled, values, (((0,), (0,)), ((), ())), preferred_element_type=f32)
        out[h * SIZE : (h + 1) * SIZE, :] = state.astype(bf16)
    pack(out, last[...])


def inner_kernel(a, b, c, g, gt, row, col, out):
    lower = row[...] >= col[...]
    for h in range(HEADS):
        query = columns((a, b, c), h * SIZE)
        keys = columns((a, b, c), WIDE + h * SIZE)
        values = columns((a, b, c), 2 * WIDE + h * SIZE)
        scores = lax.dot_general(query, keys, (((1,), (1,)), ((), ())), preferred_element_type=f32)
        lagged = g[:, h : h + 1] - gt[h : h + 1, :]
        probs = jnp.where(lower, scores * jnp.exp(jnp.minimum(lagged, 0.0)), 0.0).astype(bf16)
        out[:, h * SIZE : (h + 1) * SIZE] = jnp.dot(probs, values, preferred_element_type=f32)


def row_kernel(at, s0, s1, s2, s3, before, total):
    refs = (s0, s1, s2, s3)
    x = at[0]
    place = [(x - k) & 3 for k in range(N_X)]
    last = [unpack(ref) for ref in refs]

    def between(k, end):
        return sum(jnp.where((place[m] > place[k]) & (place[m] < end), last[m], 0.0) for m in range(N_X))

    reach = [jnp.where(place[k] < x, jnp.exp(between(k, x)), 0.0) for k in range(N_X)]
    whole = [jnp.exp(between(k, N_X)) for k in range(N_X)]
    for h in range(HEADS):
        rows = slice(h * SIZE, (h + 1) * SIZE)
        states = [ref[rows, :].astype(f32) for ref in refs]
        before[rows, :] = sum(states[k] * reach[k][h : h + 1] for k in range(1, N_X))
        total[rows, :] = sum(states[k] * whole[k][h : h + 1] for k in range(N_X)).astype(bf16)
    pack(total, last[0] + last[1] + last[2] + last[3])
    lead = sum(jnp.where(place[k] < x, last[k], 0.0) for k in range(1, N_X))
    before[WIDE:, :] = jnp.concatenate([lead, lead], axis=0)


def normed_kernel(before, t1, t2, t3, a, b, c, g, inner, gain, out):
    lead = jnp.exp(before[WIDE : WIDE + HEADS, :])
    r1, r2 = unpack(t1), unpack(t2)
    reach2, reach3 = jnp.exp(r1), jnp.exp(r1 + r2)
    for h in range(HEADS):
        rows = slice(h * SIZE, (h + 1) * SIZE)
        one = slice(h, h + 1)
        earlier = (
            t1[rows, :].astype(f32) + t2[rows, :].astype(f32) * reach2[one] + t3[rows, :].astype(f32) * reach3[one]
        )
        carried = (earlier * lead[one] + before[rows, :]).astype(bf16)
        query = columns((a, b, c), h * SIZE).astype(f32)
        scaled = (query * jnp.exp(g[:, one])).astype(bf16)
        mixed = inner[:, rows] + jnp.dot(scaled, carried, preferred_element_type=f32)
        scale = lax.rsqrt(jnp.mean(mixed * mixed, axis=-1, keepdims=True) + norm_eps)
        out[:, rows] = (mixed * scale * gain[:, rows]).astype(bf16)


def whole_call(kernel, args, outs, name, flops, scalars=0):
    nbytes = sum(a.size * a.dtype.itemsize for a in args)
    return pl.pallas_call(
        kernel,
        out_shape=outs,
        in_specs=[pl.BlockSpec(memory_space=pltpu.SMEM)] * scalars
        + [pl.BlockSpec(memory_space=pltpu.VMEM)] * (len(args) - scalars),
        out_specs=jax.tree.map(lambda _: pl.BlockSpec(memory_space=pltpu.VMEM), outs),
        compiler_params=params(),
        cost_estimate=cost(flops, nbytes),
        name=name,
    )(*args)


def project_part(rows, w, outs, m, start):
    width = w.shape[2]
    part = jnp.dot(rows, w[m], preferred_element_type=f32).astype(bf16)
    for i, out in enumerate(outs):
        out[:, start + m * width : start + (m + 1) * width] = part[i * 64 : (i + 1) * 64]


def project_first_kernel(base, start, normed, w, own, sib, held, sems):
    per = held.shape[0] // 4
    copies = [
        pltpu.make_async_copy(w.at[pl.ds(base + i * per, per)], held.at[pl.ds(i * per, per)], sems.at[i])
        for i in range(4)
    ]
    for copy in copies:
        copy.start()
    rows = normed[start : start + 128, :]
    for i in range(4):
        copies[i].wait()
        for m in range(i * per, (i + 1) * per):
            project_part(rows, held, (own, sib), m, 0)


def project_kernel(blocks, normed, w1, w2, *outs):
    rows = jnp.concatenate([normed[64 * b : 64 * b + 64, :] for b in blocks], axis=0)
    for m in range(w1.shape[0]):
        project_part(rows, w1, outs, m, 0)
        project_part(rows, w2, outs, m, outs[0].shape[1] // 2)


def project_first(normed, w, base, count, start):
    _, depth, width = w.shape
    vmem = pl.BlockSpec(memory_space=pltpu.VMEM)
    half = jax.ShapeDtypeStruct((64, count * width), bf16)
    return pl.pallas_call(
        functools.partial(project_first_kernel, base, start),
        out_shape=[half, half, pltpu.VMEM((count, depth, width), bf16)],
        in_specs=[vmem, pl.BlockSpec(memory_space=pltpu.HBM)],
        out_specs=[vmem] * 3,
        scratch_shapes=[pltpu.SemaphoreType.DMA((4,))],
        compiler_params=params(),
        cost_estimate=cost(256 * depth * count * width, 2 * depth * count * width),
        name="project",
    )(normed, pltpu.with_memory_space_constraint(w, pltpu.HBM))


def project(normed, w1, w2, blocks):
    n_ctx, depth, width = w1.shape
    n_ctx += w2.shape[0]
    vmem = pl.BlockSpec(memory_space=pltpu.VMEM)
    n = len(blocks)
    return pl.pallas_call(
        functools.partial(project_kernel, blocks),
        out_shape=[jax.ShapeDtypeStruct((64, n_ctx * width), bf16)] * n,
        in_specs=[vmem] * 3,
        out_specs=[vmem] * n,
        compiler_params=params(),
        cost_estimate=cost(2 * 64 * n * depth * n_ctx * width, 2 * depth * n_ctx * width),
        name="project",
    )(normed, w1, w2)


def gather_kernel(own, sib, up_plain, down_plain, out):
    mid = up_plain.shape[1]
    for start, other in ((0, down_plain), (mid, up_plain)):
        at = slice(start, start + mid)
        out[:, at] = own[:, at].astype(f32) + sib[:, at].astype(f32) + other[...].astype(f32)


def final_kernel(partial, up_sum, down_sum, out):
    mid = up_sum.shape[1]
    for start, other in ((0, up_sum), (mid, down_sum)):
        at = slice(start, start + mid)
        out[:, at] = (partial[:, at] + other[...].astype(f32)).astype(bf16)


def after(value, *others):
    return lax.optimization_barrier((value, *others))[0]


def plus(*terms):
    total = terms[0].astype(f32)
    for term in terms[1:]:
        total = total + term.astype(f32)
    return total.astype(bf16)


def body(activations, w_qkv, log_decay, gain, w_out):
    tp, ctx = lax.axis_index("tp"), lax.axis_index("ctx")
    y, core = tp // 2, tp % 2
    at = (ctx % N_X).astype(jnp.int32).reshape(1)
    w_all = lax.all_gather(w_out, "ctx", axis=0)

    cumul = jnp.cumsum(log_decay.T, axis=1)
    last = jnp.broadcast_to(cumul[:, -1:], (HEADS, SIZE))
    gt = jnp.roll(cumul.reshape(HEADS, N_Y, 2, 64), -y, axis=1)
    gt = jnp.where(core == 0, gt, gt[:, :, ::-1])
    gt = jnp.concatenate([gt[:, chip, half] for chip, half in PLACES], axis=1)
    g = gt.T
    chip, half = (jnp.array(np.repeat(np.array(p), 64), jnp.int32) for p in zip(*PLACES))
    pos = ((chip + y) & 3) * 128 + ((half + core) & 1) * 64 + jnp.arange(512, dtype=jnp.int32) % 64

    depth = activations.shape[1]
    mid = depth // 2
    low = activations[:, :mid]
    high = after(activations, low)[:, mid:]
    left_low, right_high = to_y(low, 1), to_y(high, -1)
    low_b, high_b = after((low, high), g, gt, last, at, pos)
    left_high, right_low = to_y(high_b, 1), to_y(low_b, -1)
    own2 = to_sibling(activations)
    own2 = after(own2, g, gt, last, at, pos)
    qkv_a, w_qkv = qkv([activations, own2], [(0, 0), (64, 0)], 128, w_qkv, True)
    left_low, right_high = after((left_low, right_high), qkv_a)
    far_low, far_high = to_y(left_low, 1), to_y(right_high, -1)
    low2, high2 = to_sibling(left_low), to_sibling(right_high)
    left_high2, right_low2 = to_sibling(left_high), to_sibling(right_low)
    near = [right_low, right_high, left_low, left_high]
    qkv_b = qkv(near, [(0, 0), (0, mid), (64, 0), (64, mid)], 128, w_qkv)
    far_low, far_high = after((far_low, far_high), qkv_b)
    rest = [right_low2, high2, low2, left_high2, far_low, far_high, to_sibling(far_low), to_sibling(far_high)]
    qkv_c = qkv(rest, [(64 * i, col) for i in range(4) for col in (0, mid)], 256, w_qkv)
    rows = (qkv_b, qkv_a, qkv_c)

    packed = jax.ShapeDtypeStruct((WIDE + 16, SIZE), bf16)
    state = whole_call(state_kernel, (*rows, g, last), packed, "state", 2 * 512 * WIDE * SIZE)
    row = [state] + [to_x(state, k) for k in range(1, N_X)]
    inner = whole_call(
        inner_kernel,
        (*rows, g, gt, pos.reshape(512, 1), pos.reshape(1, 512)),
        jax.ShapeDtypeStruct((512, WIDE), f32),
        "inner",
        4 * 512 * 512 * WIDE,
    )
    row = after(row, inner)
    before, total = whole_call(
        row_kernel, (at, *row), (jax.ShapeDtypeStruct((WIDE + 8, SIZE), f32), packed), "row", 10 * WIDE * SIZE, 1
    )
    totals = [to_z(total, k) for k in range(1, N_Z)]
    normed = whole_call(
        normed_kernel,
        (before, *totals, *rows, g, inner, gain.reshape(1, WIDE)),
        jax.ShapeDtypeStruct((512, WIDE), bf16),
        "normed",
        2 * 512 * WIDE * SIZE,
    )

    n = w_all.shape[0] // 2
    low_own, low_sib, w1 = project_first(normed, w_all, 0, n, 384)
    low_sib = to_sibling(low_sib)
    high_own, high_sib, w2 = project_first(after(normed, w1), w_all, n, n, 384)
    high_sib = to_sibling(high_sib)
    near_parts = project(after(normed, high_own), w1, w2, (0, 4, 1, 5))
    low_sib, high_sib = after((low_sib, high_sib), near_parts)
    far_low, far_high = plus(low_own, low_sib), plus(high_own, high_sib)
    from_l, from_r = to_y(far_low, 1), to_y(far_high, -1)
    up_own, up_sib, down_own, down_sib = near_parts
    up_sib, down_sib = to_sibling(up_sib), to_sibling(down_sib)
    up_plain = plus(up_own[:, mid:], up_sib[:, mid:])
    down_plain = plus(down_own[:, :mid], down_sib[:, :mid])
    normed = after(normed, up_plain, down_plain)
    up_plain, down_plain = to_y(up_plain, 1), to_y(down_plain, -1)
    here_own, here_sib = project(normed, w1, w2, (2, 3))
    from_l, from_r = after((from_l, from_r), here_own)
    up_sum = to_y(plus(up_own[:, :mid], up_sib[:, :mid], from_l), 1)
    down_sum = to_y(plus(down_own[:, mid:], down_sib[:, mid:], from_r), -1)
    here_sib = to_sibling(here_sib)
    partial = whole_call(
        gather_kernel,
        (here_own, here_sib, up_plain, down_plain),
        jax.ShapeDtypeStruct((64, depth), f32),
        "gather",
        3 * 64 * depth,
    )
    up_sum, down_sum = after((up_sum, down_sum), partial)
    return whole_call(
        final_kernel, (partial, up_sum, down_sum), jax.ShapeDtypeStruct((64, depth), bf16), "final", 64 * depth
    )


def solution(mesh):
    in_specs = (
        P(("ctx", "tp"), None),
        P(None, None, "tp"),
        P("ctx", "tp"),
        P("tp"),
        P("tp", "ctx"),
    )
    out_specs = P(("ctx", "tp"), None)
    return jax.shard_map(body, mesh=mesh, in_specs=in_specs, out_specs=out_specs, check_vma=False)
```

```python
import functools

import jax
import jax.numpy as jnp
import numpy as np
from jax import lax
from jax.experimental import pallas as pl
from jax.experimental.pallas import tpu as pltpu
from jax.sharding import PartitionSpec as P

norm_eps = 1e-06
f32, bf16 = jnp.float32, jnp.bfloat16
HEADS, SIZE = 4, 128
WIDE = HEADS * SIZE
N_X = N_Z = N_Y = 4
FAR = 384
PLACES = ((1, 0), (3, 0), (0, 0), (0, 1), (1, 1), (3, 1), (2, 0), (2, 1))
SHARE = 0.01
VMEM_LIMIT = 24 * 2**20


def params(**kw):
    return pltpu.CompilerParams(vmem_limit_bytes=VMEM_LIMIT, **kw)


def cost(flops, nbytes):
    return pl.CostEstimate(flops=int(flops * SHARE), bytes_accessed=int(nbytes * SHARE), transcendentals=0)


def to_y(a, k):
    return lax.ppermute(a, "tp", [(i, (i // 2 + k) % N_Y * 2 + i % 2) for i in range(2 * N_Y)])


def to_sibling(a):
    return lax.ppermute(a, "tp", [(i, i ^ 1) for i in range(2 * N_Y)])


def to_x(a, k):
    return lax.ppermute(a, "ctx", [(j, j // N_X * N_X + (j + k) % N_X) for j in range(N_X * N_Z)])


def to_z(a, k):
    return lax.ppermute(a, "ctx", [(j, j + N_X * k) for j in range(N_X * N_Z) if j // N_X + k < N_Z])


def place_rows(pieces, layout, rows):
    for piece, (row, col) in zip(pieces, layout):
        rows[row : row + piece.shape[0], col : col + piece.shape[1]] = piece[...]


def activate(member, acc):
    return (acc if member == 2 else acc / (1.0 + jnp.exp(-acc))).astype(bf16)


def qkv_first_kernel(layout, *refs):
    n = len(layout)
    pieces, w, out, held, rows, sems = refs[:n], refs[n], *refs[n + 1 :]
    depth = w.shape[1]
    cut = depth // 4
    copies = [
        [
            pltpu.make_async_copy(w.at[m, pl.ds(k * cut, cut)], held.at[m, pl.ds(k * cut, cut)], sems.at[m, k])
            for k in range(4)
        ]
        for m in range(3)
    ]
    for m in range(3):
        for k in range(4):
            copies[m][k].start()
    place_rows(pieces, layout, rows)
    for m in range(3):
        acc = None
        for k in range(4):
            copies[m][k].wait()
            part = jnp.dot(
                rows[:, k * cut : (k + 1) * cut], held[m, k * cut : (k + 1) * cut], preferred_element_type=f32
            )
            acc = part if acc is None else acc + part
        out[:, m * WIDE : (m + 1) * WIDE] = activate(m, acc)


def qkv_kernel(layout, *refs):
    n = len(layout)
    pieces, w, out, rows = refs[:n], refs[n], refs[n + 1], refs[n + 2]
    place_rows(pieces, layout, rows)
    tile = 256
    for m in range(3):
        for start in range(0, WIDE, tile):
            acc = jnp.dot(rows[...], w[m, :, start : start + tile], preferred_element_type=f32)
            out[:, m * WIDE + start : m * WIDE + start + tile] = activate(m, acc)


def qkv(pieces, layout, count, w, first=False):
    depth = w.shape[1]
    out = jax.ShapeDtypeStruct((count, 3 * WIDE), bf16)
    vmem = pl.BlockSpec(memory_space=pltpu.VMEM)
    return pl.pallas_call(
        functools.partial(qkv_first_kernel if first else qkv_kernel, layout),
        out_shape=(out, pltpu.VMEM(w.shape, bf16)) if first else out,
        in_specs=[vmem] * len(pieces) + [pl.BlockSpec(memory_space=pltpu.HBM) if first else vmem],
        out_specs=(vmem, vmem) if first else vmem,
        scratch_shapes=[pltpu.VMEM((count, depth), bf16)] + ([pltpu.SemaphoreType.DMA((3, 4))] if first else []),
        compiler_params=params(),
        cost_estimate=cost(2 * count * depth * 3 * WIDE, 3 * WIDE * depth * 2),
        name="qkv",
    )(*pieces, w)


def columns(refs, start):
    return jnp.concatenate([ref[:, start : start + SIZE] for ref in refs], axis=0)


def pack(out, last):
    high = last.astype(bf16).astype(f32)
    mid = (last - high).astype(bf16).astype(f32)
    low = last - high - mid
    out[WIDE:, :] = jnp.concatenate([high, mid, low, jnp.zeros_like(low)], axis=0).astype(bf16)


def unpack(ref):
    tail = ref[WIDE:, :].astype(f32)
    return tail[0:4] + tail[4:8] + tail[8:12]


def state_kernel(a, b, c, d, g, last, out):
    for h in range(HEADS):
        keys = columns((a, b, c, d), WIDE + h * SIZE).astype(f32)
        values = columns((a, b, c, d), 2 * WIDE + h * SIZE)
        scaled = (keys * jnp.exp(last[h : h + 1, 0:1] - g[:, h : h + 1])).astype(bf16)
        state = lax.dot_general(scaled, values, (((0,), (0,)), ((), ())), preferred_element_type=f32)
        out[h * SIZE : (h + 1) * SIZE, :] = state.astype(bf16)
    pack(out, last[...])


def inner_kernel(a, b, c, d, g, gt, row, col, out):
    lower = row[...] >= col[...]
    for h in range(HEADS):
        query = columns((a, b, c, d), h * SIZE)
        keys = columns((a, b, c, d), WIDE + h * SIZE)
        values = columns((a, b, c, d), 2 * WIDE + h * SIZE)
        scores = lax.dot_general(query, keys, (((1,), (1,)), ((), ())), preferred_element_type=f32)
        lagged = g[:, h : h + 1] - gt[h : h + 1, :]
        probs = jnp.where(lower, scores * jnp.exp(jnp.minimum(lagged, 0.0)), 0.0).astype(bf16)
        out[:, h * SIZE : (h + 1) * SIZE] = jnp.dot(probs, values, preferred_element_type=f32)


def row_kernel(at, s0, s1, s2, s3, before, total):
    refs = (s0, s1, s2, s3)
    x = at[0]
    place = [(x - k) & 3 for k in range(N_X)]
    last = [unpack(ref) for ref in refs]

    def between(k, end):
        return sum(jnp.where((place[m] > place[k]) & (place[m] < end), last[m], 0.0) for m in range(N_X))

    reach = [jnp.where(place[k] < x, jnp.exp(between(k, x)), 0.0) for k in range(N_X)]
    whole = [jnp.exp(between(k, N_X)) for k in range(N_X)]
    for h in range(HEADS):
        rows = slice(h * SIZE, (h + 1) * SIZE)
        states = [ref[rows, :].astype(f32) for ref in refs]
        before[rows, :] = sum(states[k] * reach[k][h : h + 1] for k in range(1, N_X))
        total[rows, :] = sum(states[k] * whole[k][h : h + 1] for k in range(N_X)).astype(bf16)
    pack(total, last[0] + last[1] + last[2] + last[3])
    lead = sum(jnp.where(place[k] < x, last[k], 0.0) for k in range(1, N_X))
    before[WIDE:, :] = jnp.concatenate([lead, lead], axis=0)


def normed_kernel(before, t1, t2, t3, a, b, c, d, g, inner, gain, w, out, own, sib, held, sems):
    per = w.shape[0] // 4
    copies = [
        pltpu.make_async_copy(w.at[pl.ds(i * per, per)], held.at[pl.ds(i * per, per)], sems.at[i]) for i in range(4)
    ]
    for copy in copies:
        copy.start()
    lead = jnp.exp(before[WIDE : WIDE + HEADS, :])
    r1, r2 = unpack(t1), unpack(t2)
    reach2, reach3 = jnp.exp(r1), jnp.exp(r1 + r2)
    for h in range(HEADS):
        rows = slice(h * SIZE, (h + 1) * SIZE)
        one = slice(h, h + 1)
        earlier = (
            t1[rows, :].astype(f32) + t2[rows, :].astype(f32) * reach2[one] + t3[rows, :].astype(f32) * reach3[one]
        )
        carried = (earlier * lead[one] + before[rows, :]).astype(bf16)
        query = columns((a, b, c, d), h * SIZE).astype(f32)
        scaled = (query * jnp.exp(g[:, one])).astype(bf16)
        mixed = inner[:, rows] + jnp.dot(scaled, carried, preferred_element_type=f32)
        scale = lax.rsqrt(jnp.mean(mixed * mixed, axis=-1, keepdims=True) + norm_eps)
        out[:, rows] = (mixed * scale * gain[:, rows]).astype(bf16)
    far = out[FAR : FAR + 128, :]
    for i in range(4):
        copies[i].wait()
        for m in range(i * per, (i + 1) * per):
            project_part(far, held, (own, sib), m)


def whole_call(kernel, args, outs, name, flops, scalars=0):
    nbytes = sum(a.size * a.dtype.itemsize for a in args)
    return pl.pallas_call(
        kernel,
        out_shape=outs,
        in_specs=[pl.BlockSpec(memory_space=pltpu.SMEM)] * scalars
        + [pl.BlockSpec(memory_space=pltpu.VMEM)] * (len(args) - scalars),
        out_specs=jax.tree.map(lambda _: pl.BlockSpec(memory_space=pltpu.VMEM), outs),
        compiler_params=params(),
        cost_estimate=cost(flops, nbytes),
        name=name,
    )(*args)


def project_part(rows, w, outs, m):
    width = w.shape[2]
    part = jnp.dot(rows, w[m], preferred_element_type=f32).astype(bf16)
    for i, out in enumerate(outs):
        out[:, m * width : (m + 1) * width] = part[i * 64 : (i + 1) * 64]


def project_kernel(blocks, normed, w, *outs):
    rows = jnp.concatenate([normed[64 * b : 64 * b + 64, :] for b in blocks], axis=0)
    for m in range(w.shape[0]):
        project_part(rows, w, outs, m)


def project(normed, w, blocks):
    n_ctx, depth, width = w.shape
    vmem = pl.BlockSpec(memory_space=pltpu.VMEM)
    n = len(blocks)
    return pl.pallas_call(
        functools.partial(project_kernel, blocks),
        out_shape=[jax.ShapeDtypeStruct((64, n_ctx * width), bf16)] * n,
        in_specs=[vmem] * 2,
        out_specs=[vmem] * n,
        compiler_params=params(),
        cost_estimate=cost(2 * 64 * n * depth * n_ctx * width, 2 * depth * n_ctx * width),
        name="project",
    )(normed, w)


def gather_kernel(own, sib, up_plain, down_plain, out):
    mid = up_plain.shape[1]
    for start, other in ((0, down_plain), (mid, up_plain)):
        at = slice(start, start + mid)
        out[:, at] = own[:, at].astype(f32) + sib[:, at].astype(f32) + other[...].astype(f32)


def final_kernel(partial, up_sum, down_sum, out):
    mid = up_sum.shape[1]
    for start, other in ((0, up_sum), (mid, down_sum)):
        at = slice(start, start + mid)
        out[:, at] = (partial[:, at] + other[...].astype(f32)).astype(bf16)


def after(value, *others):
    return lax.optimization_barrier((value, *others))[0]


def plus(*terms):
    total = terms[0].astype(f32)
    for term in terms[1:]:
        total = total + term.astype(f32)
    return total.astype(bf16)


def body(activations, w_qkv, log_decay, gain, w_out):
    tp, ctx = lax.axis_index("tp"), lax.axis_index("ctx")
    y, core = tp // 2, tp % 2
    at = (ctx % N_X).astype(jnp.int32).reshape(1)
    w_all = lax.all_gather(w_out, "ctx", axis=0)

    cumul = jnp.cumsum(log_decay.T, axis=1)
    last = jnp.broadcast_to(cumul[:, -1:], (HEADS, SIZE))
    gt = jnp.roll(cumul.reshape(HEADS, N_Y, 2, 64), -y, axis=1)
    gt = jnp.where(core == 0, gt, gt[:, :, ::-1])
    gt = jnp.concatenate([gt[:, chip, half] for chip, half in PLACES], axis=1)
    g = gt.T
    chip, half = (jnp.array(np.repeat(np.array(p), 64), jnp.int32) for p in zip(*PLACES))
    pos = ((chip + y) & 3) * 128 + ((half + core) & 1) * 64 + jnp.arange(512, dtype=jnp.int32) % 64

    depth = activations.shape[1]
    mid = depth // 2
    low = activations[:, :mid]
    high = after(activations, low)[:, mid:]
    left_low, right_high = to_y(low, 1), to_y(high, -1)
    low_b, high_b = after((low, high), g, gt, last, at, pos)
    left_high, right_low = to_y(high_b, 1), to_y(low_b, -1)
    own2 = to_sibling(activations)
    far_low, far_high = to_y(left_low, 1), to_y(right_high, -1)
    own2 = after(own2, g, gt, last, at, pos, left_low, right_high)
    qkv_a, w_qkv = qkv([activations, own2], [(0, 0), (64, 0)], 128, w_qkv, True)
    low2, high2 = to_sibling(left_low), to_sibling(right_high)
    left_high, right_low = after((left_high, right_low), qkv_a)
    left_high2, right_low2 = to_sibling(left_high), to_sibling(right_low)
    halves = [(0, 0), (0, mid), (64, 0), (64, mid)]
    qkv_b = qkv([right_low, right_high, left_low, left_high], halves, 128, w_qkv)
    far_low, far_high = after((far_low, far_high), qkv_b)
    far_low2, far_high2 = to_sibling(far_low), to_sibling(far_high)
    near2 = after([right_low2, high2, low2, left_high2], far_low, far_high)
    qkv_c = qkv(near2, halves, 128, w_qkv)
    far_low2, far_high2 = after((far_low2, far_high2), qkv_c)
    qkv_d = qkv([far_low, far_high, far_low2, far_high2], halves, 128, w_qkv)
    rows = (qkv_b, qkv_a, qkv_c, qkv_d)

    packed = jax.ShapeDtypeStruct((WIDE + 16, SIZE), bf16)
    state = whole_call(state_kernel, (*rows, g, last), packed, "state", 2 * 512 * WIDE * SIZE)
    row = [state] + [to_x(state, k) for k in range(1, N_X)]
    inner = whole_call(
        inner_kernel,
        (*rows, g, gt, pos.reshape(512, 1), pos.reshape(1, 512)),
        jax.ShapeDtypeStruct((512, WIDE), f32),
        "inner",
        4 * 512 * 512 * WIDE,
    )
    row = after(row, inner)
    before, total = whole_call(
        row_kernel, (at, *row), (jax.ShapeDtypeStruct((WIDE + 8, SIZE), f32), packed), "row", 10 * WIDE * SIZE, 1
    )
    totals = [to_z(total, k) for k in range(1, N_Z)]
    vmem = pl.BlockSpec(memory_space=pltpu.VMEM)
    args = (before, *totals, *rows, g, inner, gain.reshape(1, WIDE))
    half = jax.ShapeDtypeStruct((64, depth), bf16)
    normed, far_own, far_sib, w = pl.pallas_call(
        normed_kernel,
        out_shape=[jax.ShapeDtypeStruct((512, WIDE), bf16), half, half, pltpu.VMEM(w_all.shape, bf16)],
        in_specs=[vmem] * len(args) + [pl.BlockSpec(memory_space=pltpu.HBM)],
        out_specs=[vmem] * 4,
        scratch_shapes=[pltpu.SemaphoreType.DMA((4,))],
        compiler_params=params(),
        cost_estimate=cost(2 * 512 * WIDE * SIZE, 2 * w_all.size),
        name="normed",
    )(*args, pltpu.with_memory_space_constraint(w_all, pltpu.HBM))

    far_sib = to_sibling(far_sib)
    near_parts = project(normed, w, (0, 4, 1, 5))
    far_sib = after(far_sib, near_parts)
    from_l = to_y(plus(far_own[:, :mid], far_sib[:, :mid]), 1)
    from_r = to_y(plus(far_own[:, mid:], far_sib[:, mid:]), -1)
    up_own, up_sib, down_own, down_sib = near_parts
    up_sib, down_sib = to_sibling(up_sib), to_sibling(down_sib)
    up_plain = plus(up_own[:, mid:], up_sib[:, mid:])
    down_plain = plus(down_own[:, :mid], down_sib[:, :mid])
    normed = after(normed, up_plain, down_plain)
    up_plain, down_plain = to_y(up_plain, 1), to_y(down_plain, -1)
    here_own, here_sib = project(normed, w, (2, 3))
    from_l, from_r = after((from_l, from_r), here_own)
    up_sum = to_y(plus(up_own[:, :mid], up_sib[:, :mid], from_l), 1)
    down_sum = to_y(plus(down_own[:, mid:], down_sib[:, mid:], from_r), -1)
    here_sib = to_sibling(here_sib)
    partial = whole_call(
        gather_kernel,
        (here_own, here_sib, up_plain, down_plain),
        jax.ShapeDtypeStruct((64, depth), f32),
        "gather",
        3 * 64 * depth,
    )
    up_sum, down_sum = after((up_sum, down_sum), partial)
    return whole_call(
        final_kernel, (partial, up_sum, down_sum), jax.ShapeDtypeStruct((64, depth), bf16), "final", 64 * depth
    )


def solution(mesh):
    in_specs = (
        P(("ctx", "tp"), None),
        P(None, None, "tp"),
        P("ctx", "tp"),
        P("tp"),
        P("tp", "ctx"),
    )
    out_specs = P(("ctx", "tp"), None)
    return jax.shard_map(body, mesh=mesh, in_specs=in_specs, out_specs=out_specs, check_vma=False)
```

```python
import functools

import jax
import jax.numpy as jnp
import numpy as np
from jax import lax
from jax.experimental import pallas as pl
from jax.experimental.pallas import tpu as pltpu
from jax.sharding import PartitionSpec as P

norm_eps = 1e-06
f32, bf16 = jnp.float32, jnp.bfloat16
HEADS, SIZE = 4, 128
WIDE = HEADS * SIZE
N_X = N_Z = N_Y = 4
FAR = 384
PLACES = ((1, 0), (3, 0), (0, 0), (0, 1), (1, 1), (3, 1), (2, 0), (2, 1))
SHARE = 0.01
VMEM_LIMIT = 24 * 2**20


def params(**kw):
    return pltpu.CompilerParams(vmem_limit_bytes=VMEM_LIMIT, **kw)


def cost(flops, nbytes):
    return pl.CostEstimate(flops=int(flops * SHARE), bytes_accessed=int(nbytes * SHARE), transcendentals=0)


def to_y(a, k):
    return lax.ppermute(a, "tp", [(i, (i // 2 + k) % N_Y * 2 + i % 2) for i in range(2 * N_Y)])


def to_sibling(a):
    return lax.ppermute(a, "tp", [(i, i ^ 1) for i in range(2 * N_Y)])


def to_x(a, k):
    return lax.ppermute(a, "ctx", [(j, j // N_X * N_X + (j + k) % N_X) for j in range(N_X * N_Z)])


def to_z(a, k):
    return lax.ppermute(a, "ctx", [(j, j + N_X * k) for j in range(N_X * N_Z) if j // N_X + k < N_Z])


def place_rows(pieces, layout, rows):
    for piece, (row, col) in zip(pieces, layout):
        rows[row : row + piece.shape[0], col : col + piece.shape[1]] = piece[...]


def activate(member, acc):
    return (acc if member == 2 else acc / (1.0 + jnp.exp(-acc))).astype(bf16)


def qkv_first_kernel(layout, *refs):
    n = len(layout)
    pieces, w, out, held, rows, sems = refs[:n], refs[n], *refs[n + 1 :]
    depth = w.shape[1]
    cut = depth // 4
    copies = [
        [
            pltpu.make_async_copy(w.at[m, pl.ds(k * cut, cut)], held.at[m, pl.ds(k * cut, cut)], sems.at[m, k])
            for k in range(4)
        ]
        for m in range(3)
    ]
    for m in range(3):
        for k in range(4):
            copies[m][k].start()
    place_rows(pieces, layout, rows)
    for m in range(3):
        acc = None
        for k in range(4):
            copies[m][k].wait()
            part = jnp.dot(
                rows[:, k * cut : (k + 1) * cut], held[m, k * cut : (k + 1) * cut], preferred_element_type=f32
            )
            acc = part if acc is None else acc + part
        out[:, m * WIDE : (m + 1) * WIDE] = activate(m, acc)


def qkv_kernel(layout, *refs):
    n = len(layout)
    pieces, w, out, rows = refs[:n], refs[n], refs[n + 1], refs[n + 2]
    place_rows(pieces, layout, rows)
    tile = 256
    for m in range(3):
        for start in range(0, WIDE, tile):
            acc = jnp.dot(rows[...], w[m, :, start : start + tile], preferred_element_type=f32)
            out[:, m * WIDE + start : m * WIDE + start + tile] = activate(m, acc)


def qkv(pieces, layout, count, w, first=False):
    depth = w.shape[1]
    out = jax.ShapeDtypeStruct((count, 3 * WIDE), bf16)
    vmem = pl.BlockSpec(memory_space=pltpu.VMEM)
    return pl.pallas_call(
        functools.partial(qkv_first_kernel if first else qkv_kernel, layout),
        out_shape=(out, pltpu.VMEM(w.shape, bf16)) if first else out,
        in_specs=[vmem] * len(pieces) + [pl.BlockSpec(memory_space=pltpu.HBM) if first else vmem],
        out_specs=(vmem, vmem) if first else vmem,
        scratch_shapes=[pltpu.VMEM((count, depth), bf16)] + ([pltpu.SemaphoreType.DMA((3, 4))] if first else []),
        compiler_params=params(),
        cost_estimate=cost(2 * count * depth * 3 * WIDE, 3 * WIDE * depth * 2),
        name="qkv",
    )(*pieces, w)


def columns(refs, start):
    return jnp.concatenate([ref[:, start : start + SIZE] for ref in refs], axis=0)


def pack(out, last):
    high = last.astype(bf16).astype(f32)
    mid = (last - high).astype(bf16).astype(f32)
    low = last - high - mid
    out[WIDE:, :] = jnp.concatenate([high, mid, low, jnp.zeros_like(low)], axis=0).astype(bf16)


def unpack(ref):
    tail = ref[WIDE:, :].astype(f32)
    return tail[0:4] + tail[4:8] + tail[8:12]


def state_kernel(a, b, c, d, g, last, out):
    for h in range(HEADS):
        keys = columns((a, b, c, d), WIDE + h * SIZE).astype(f32)
        values = columns((a, b, c, d), 2 * WIDE + h * SIZE)
        scaled = (keys * jnp.exp(last[h : h + 1, 0:1] - g[:, h : h + 1])).astype(bf16)
        state = lax.dot_general(scaled, values, (((0,), (0,)), ((), ())), preferred_element_type=f32)
        out[h * SIZE : (h + 1) * SIZE, :] = state.astype(bf16)
    pack(out, last[...])


def inner_kernel(a, b, c, d, g, gt, row, col, out):
    lower = row[...] >= col[...]
    for h in range(HEADS):
        query = columns((a, b, c, d), h * SIZE)
        keys = columns((a, b, c, d), WIDE + h * SIZE)
        values = columns((a, b, c, d), 2 * WIDE + h * SIZE)
        scores = lax.dot_general(query, keys, (((1,), (1,)), ((), ())), preferred_element_type=f32)
        lagged = g[:, h : h + 1] - gt[h : h + 1, :]
        probs = jnp.where(lower, scores * jnp.exp(jnp.minimum(lagged, 0.0)), 0.0).astype(bf16)
        out[:, h * SIZE : (h + 1) * SIZE] = jnp.dot(probs, values, preferred_element_type=f32)


def row_kernel(at, s0, s1, s2, s3, before, total):
    refs = (s0, s1, s2, s3)
    x = at[0]
    place = [(x - k) & 3 for k in range(N_X)]
    last = [unpack(ref) for ref in refs]

    def between(k, end):
        return sum(jnp.where((place[m] > place[k]) & (place[m] < end), last[m], 0.0) for m in range(N_X))

    reach = [jnp.where(place[k] < x, jnp.exp(between(k, x)), 0.0) for k in range(N_X)]
    whole = [jnp.exp(between(k, N_X)) for k in range(N_X)]
    for h in range(HEADS):
        rows = slice(h * SIZE, (h + 1) * SIZE)
        states = [ref[rows, :].astype(f32) for ref in refs]
        before[rows, :] = sum(states[k] * reach[k][h : h + 1] for k in range(1, N_X))
        total[rows, :] = sum(states[k] * whole[k][h : h + 1] for k in range(N_X)).astype(bf16)
    pack(total, last[0] + last[1] + last[2] + last[3])
    lead = sum(jnp.where(place[k] < x, last[k], 0.0) for k in range(1, N_X))
    before[WIDE:, :] = jnp.concatenate([lead, lead], axis=0)


def normed_kernel(before, t1, t2, t3, a, b, c, d, g, inner, gain, w, out, own, sib, held, sems):
    per = w.shape[0] // 4
    copies = [
        pltpu.make_async_copy(w.at[pl.ds(i * per, per)], held.at[pl.ds(i * per, per)], sems.at[i]) for i in range(4)
    ]
    for copy in copies:
        copy.start()
    lead = jnp.exp(before[WIDE : WIDE + HEADS, :])
    r1, r2 = unpack(t1), unpack(t2)
    reach2, reach3 = jnp.exp(r1), jnp.exp(r1 + r2)
    for h in range(HEADS):
        rows = slice(h * SIZE, (h + 1) * SIZE)
        one = slice(h, h + 1)
        earlier = (
            t1[rows, :].astype(f32) + t2[rows, :].astype(f32) * reach2[one] + t3[rows, :].astype(f32) * reach3[one]
        )
        carried = (earlier * lead[one] + before[rows, :]).astype(bf16)
        query = columns((a, b, c, d), h * SIZE).astype(f32)
        scaled = (query * jnp.exp(g[:, one])).astype(bf16)
        mixed = inner[:, rows] + jnp.dot(scaled, carried, preferred_element_type=f32)
        scale = lax.rsqrt(jnp.mean(mixed * mixed, axis=-1, keepdims=True) + norm_eps)
        out[:, rows] = (mixed * scale * gain[:, rows]).astype(bf16)
    far = out[FAR : FAR + 128, :]
    for i in range(4):
        copies[i].wait()
        for m in range(i * per, (i + 1) * per):
            project_part(far, held, (own, sib), m)


def whole_call(kernel, args, outs, name, flops, scalars=0):
    nbytes = sum(a.size * a.dtype.itemsize for a in args)
    return pl.pallas_call(
        kernel,
        out_shape=outs,
        in_specs=[pl.BlockSpec(memory_space=pltpu.SMEM)] * scalars
        + [pl.BlockSpec(memory_space=pltpu.VMEM)] * (len(args) - scalars),
        out_specs=jax.tree.map(lambda _: pl.BlockSpec(memory_space=pltpu.VMEM), outs),
        compiler_params=params(),
        cost_estimate=cost(flops, nbytes),
        name=name,
    )(*args)


def project_part(rows, w, outs, m):
    width = w.shape[2]
    part = jnp.dot(rows, w[m], preferred_element_type=f32).astype(bf16)
    for i, out in enumerate(outs):
        out[:, m * width : (m + 1) * width] = part[i * 64 : (i + 1) * 64]


def project_kernel(blocks, normed, w, *outs):
    rows = jnp.concatenate([normed[64 * b : 64 * b + 64, :] for b in blocks], axis=0)
    for m in range(w.shape[0]):
        project_part(rows, w, outs, m)


def project(normed, w, blocks):
    n_ctx, depth, width = w.shape
    vmem = pl.BlockSpec(memory_space=pltpu.VMEM)
    n = len(blocks)
    return pl.pallas_call(
        functools.partial(project_kernel, blocks),
        out_shape=[jax.ShapeDtypeStruct((64, n_ctx * width), bf16)] * n,
        in_specs=[vmem] * 2,
        out_specs=[vmem] * n,
        compiler_params=params(),
        cost_estimate=cost(2 * 64 * n * depth * n_ctx * width, 2 * depth * n_ctx * width),
        name="project",
    )(normed, w)


def gather_kernel(own, sib, up_plain, down_plain, out):
    mid = up_plain.shape[1]
    for start, other in ((0, down_plain), (mid, up_plain)):
        at = slice(start, start + mid)
        out[:, at] = own[:, at].astype(f32) + sib[:, at].astype(f32) + other[...].astype(f32)


def final_kernel(partial, up_sum, down_sum, out):
    mid = up_sum.shape[1]
    for start, other in ((0, up_sum), (mid, down_sum)):
        at = slice(start, start + mid)
        out[:, at] = (partial[:, at] + other[...].astype(f32)).astype(bf16)


def after(value, *others):
    return lax.optimization_barrier((value, *others))[0]


def plus(*terms):
    total = terms[0].astype(f32)
    for term in terms[1:]:
        total = total + term.astype(f32)
    return total.astype(bf16)


def body(activations, w_qkv, log_decay, gain, w_out):
    tp, ctx = lax.axis_index("tp"), lax.axis_index("ctx")
    y, core = tp // 2, tp % 2
    at = (ctx % N_X).astype(jnp.int32).reshape(1)
    w_all = lax.all_gather(w_out, "ctx", axis=0)

    cumul = jnp.cumsum(log_decay.T, axis=1)
    last = jnp.broadcast_to(cumul[:, -1:], (HEADS, SIZE))
    gt = jnp.roll(cumul.reshape(HEADS, N_Y, 2, 64), -y, axis=1)
    gt = jnp.where(core == 0, gt, gt[:, :, ::-1])
    gt = jnp.concatenate([gt[:, chip, half] for chip, half in PLACES], axis=1)
    g = gt.T
    chip, half = (jnp.array(np.repeat(np.array(p), 64), jnp.int32) for p in zip(*PLACES))
    pos = ((chip + y) & 3) * 128 + ((half + core) & 1) * 64 + jnp.arange(512, dtype=jnp.int32) % 64

    depth = activations.shape[1]
    mid = depth // 2
    low = activations[:, :mid]
    high = after(activations, low)[:, mid:]
    left_low, right_high = to_y(low, 1), to_y(high, -1)
    low_b, high_b = after((low, high), g, gt, last, at, pos)
    left_high, right_low = to_y(high_b, 1), to_y(low_b, -1)
    own2 = to_sibling(activations)
    own2 = after(own2, g, gt, last, at, pos)
    qkv_a, w_qkv = qkv([activations, own2], [(0, 0), (64, 0)], 128, w_qkv, True)
    left_low, right_high = after((left_low, right_high), qkv_a)
    far_low, far_high = to_y(left_low, 1), to_y(right_high, -1)
    low2, high2 = to_sibling(left_low), to_sibling(right_high)
    left_high2, right_low2 = to_sibling(left_high), to_sibling(right_low)
    halves = [(0, 0), (0, mid), (64, 0), (64, mid)]
    near = after((right_low, right_high, left_low, left_high), low2, high2)
    qkv_b = qkv(near, halves, 128, w_qkv)
    far_low, far_high = after((far_low, far_high), qkv_b)
    far_low2, far_high2 = to_sibling(far_low), to_sibling(far_high)
    near2 = after([right_low2, high2, low2, left_high2], far_low, far_high)
    qkv_c = qkv(near2, halves, 128, w_qkv)
    far_low2, far_high2 = after((far_low2, far_high2), qkv_c)
    qkv_d = qkv([far_low, far_high, far_low2, far_high2], halves, 128, w_qkv)
    rows = (qkv_b, qkv_a, qkv_c, qkv_d)

    packed = jax.ShapeDtypeStruct((WIDE + 16, SIZE), bf16)
    state = whole_call(state_kernel, (*rows, g, last), packed, "state", 2 * 512 * WIDE * SIZE)
    row = [state] + [to_x(state, k) for k in range(1, N_X)]
    inner = whole_call(
        inner_kernel,
        (*rows, g, gt, pos.reshape(512, 1), pos.reshape(1, 512)),
        jax.ShapeDtypeStruct((512, WIDE), f32),
        "inner",
        4 * 512 * 512 * WIDE,
    )
    row = after(row, inner)
    before, total = whole_call(
        row_kernel, (at, *row), (jax.ShapeDtypeStruct((WIDE + 8, SIZE), f32), packed), "row", 10 * WIDE * SIZE, 1
    )
    totals = [to_z(total, k) for k in range(1, N_Z)]
    vmem = pl.BlockSpec(memory_space=pltpu.VMEM)
    args = (before, *totals, *rows, g, inner, gain.reshape(1, WIDE))
    half = jax.ShapeDtypeStruct((64, depth), bf16)
    normed, far_own, far_sib, w = pl.pallas_call(
        normed_kernel,
        out_shape=[jax.ShapeDtypeStruct((512, WIDE), bf16), half, half, pltpu.VMEM(w_all.shape, bf16)],
        in_specs=[vmem] * len(args) + [pl.BlockSpec(memory_space=pltpu.HBM)],
        out_specs=[vmem] * 4,
        scratch_shapes=[pltpu.SemaphoreType.DMA((4,))],
        compiler_params=params(),
        cost_estimate=cost(2 * 512 * WIDE * SIZE, 2 * w_all.size),
        name="normed",
    )(*args, pltpu.with_memory_space_constraint(w_all, pltpu.HBM))

    far_sib = to_sibling(far_sib)
    near_parts = project(normed, w, (0, 4, 1, 5))
    far_sib = after(far_sib, near_parts)
    far = plus(far_own[:, :mid], far_sib[:, :mid]), plus(far_own[:, mid:], far_sib[:, mid:])
    from_l, from_r = to_y(far[0], 1), to_y(far[1], -1)
    up_own, up_sib, down_own, down_sib = after(near_parts, *far)
    up_sib, down_sib = to_sibling(up_sib), to_sibling(down_sib)
    up_plain = plus(up_own[:, mid:], up_sib[:, mid:])
    down_plain = plus(down_own[:, :mid], down_sib[:, :mid])
    normed = after(normed, up_plain, down_plain)
    up_plain, down_plain = to_y(up_plain, 1), to_y(down_plain, -1)
    here_own, here_sib = project(normed, w, (2, 3))
    from_l, from_r = after((from_l, from_r), here_own)
    up_sum = to_y(plus(up_own[:, :mid], up_sib[:, :mid], from_l), 1)
    down_sum = to_y(plus(down_own[:, mid:], down_sib[:, mid:], from_r), -1)
    here_sib = to_sibling(here_sib)
    partial = whole_call(
        gather_kernel,
        (here_own, here_sib, up_plain, down_plain),
        jax.ShapeDtypeStruct((64, depth), f32),
        "gather",
        3 * 64 * depth,
    )
    up_sum, down_sum = after((up_sum, down_sum), partial)
    return whole_call(
        final_kernel, (partial, up_sum, down_sum), jax.ShapeDtypeStruct((64, depth), bf16), "final", 64 * depth
    )


def solution(mesh):
    in_specs = (
        P(("ctx", "tp"), None),
        P(None, None, "tp"),
        P("ctx", "tp"),
        P("tp"),
        P("tp", "ctx"),
    )
    out_specs = P(("ctx", "tp"), None)
    return jax.shard_map(body, mesh=mesh, in_specs=in_specs, out_specs=out_specs, check_vma=False)
```

```python
import functools

import jax
import jax.numpy as jnp
import numpy as np
from jax import lax
from jax.experimental import pallas as pl
from jax.experimental.pallas import tpu as pltpu
from jax.sharding import PartitionSpec as P

norm_eps = 1e-06
f32, bf16 = jnp.float32, jnp.bfloat16
HEADS, SIZE = 4, 128
WIDE = HEADS * SIZE
N_X = N_Z = N_Y = 4
FAR = 384
PLACES = ((1, 0), (3, 0), (0, 0), (0, 1), (1, 1), (3, 1), (2, 0), (2, 1))
SHARE = 0.01
VMEM_LIMIT = 20 * 2**20


def params(**kw):
    return pltpu.CompilerParams(vmem_limit_bytes=VMEM_LIMIT, **kw)


def cost(flops, nbytes):
    return pl.CostEstimate(flops=int(flops * SHARE), bytes_accessed=int(nbytes * SHARE), transcendentals=0)


def to_y(a, k):
    return lax.ppermute(a, "tp", [(i, (i // 2 + k) % N_Y * 2 + i % 2) for i in range(2 * N_Y)])


def to_sibling(a):
    return lax.ppermute(a, "tp", [(i, i ^ 1) for i in range(2 * N_Y)])


def to_x(a, k):
    return lax.ppermute(a, "ctx", [(j, j // N_X * N_X + (j + k) % N_X) for j in range(N_X * N_Z)])


def to_z(a, k):
    return lax.ppermute(a, "ctx", [(j, j + N_X * k) for j in range(N_X * N_Z) if j // N_X + k < N_Z])


def place_rows(pieces, layout, rows):
    for piece, (row, col) in zip(pieces, layout):
        rows[row : row + piece.shape[0], col : col + piece.shape[1]] = piece[...]


def activate(member, acc):
    return (acc if member == 2 else acc / (1.0 + jnp.exp(-acc))).astype(bf16)


def qkv_first_kernel(layout, *refs):
    n = len(layout)
    pieces, w, out, held, rows, sems = refs[:n], refs[n], *refs[n + 1 :]
    depth = w.shape[1]
    cut = depth // 4
    copies = [
        [
            pltpu.make_async_copy(w.at[m, pl.ds(k * cut, cut)], held.at[m, pl.ds(k * cut, cut)], sems.at[m, k])
            for k in range(4)
        ]
        for m in range(3)
    ]
    for m in range(3):
        for k in range(4):
            copies[m][k].start()
    place_rows(pieces, layout, rows)
    for m in range(3):
        acc = None
        for k in range(4):
            copies[m][k].wait()
            part = jnp.dot(
                rows[:, k * cut : (k + 1) * cut], held[m, k * cut : (k + 1) * cut], preferred_element_type=f32
            )
            acc = part if acc is None else acc + part
        out[:, m * WIDE : (m + 1) * WIDE] = activate(m, acc)


def qkv_kernel(layout, *refs):
    n = len(layout)
    pieces, w, out, rows = refs[:n], refs[n], refs[n + 1], refs[n + 2]
    place_rows(pieces, layout, rows)
    tile = 256
    for m in range(3):
        for start in range(0, WIDE, tile):
            acc = jnp.dot(rows[...], w[m, :, start : start + tile], preferred_element_type=f32)
            out[:, m * WIDE + start : m * WIDE + start + tile] = activate(m, acc)


def qkv(pieces, layout, count, w, first=False):
    depth = w.shape[1]
    out = jax.ShapeDtypeStruct((count, 3 * WIDE), bf16)
    vmem = pl.BlockSpec(memory_space=pltpu.VMEM)
    return pl.pallas_call(
        functools.partial(qkv_first_kernel if first else qkv_kernel, layout),
        out_shape=(out, pltpu.VMEM(w.shape, bf16)) if first else out,
        in_specs=[vmem] * len(pieces) + [pl.BlockSpec(memory_space=pltpu.HBM) if first else vmem],
        out_specs=(vmem, vmem) if first else vmem,
        scratch_shapes=[pltpu.VMEM((count, depth), bf16)] + ([pltpu.SemaphoreType.DMA((3, 4))] if first else []),
        compiler_params=params(),
        cost_estimate=cost(2 * count * depth * 3 * WIDE, 3 * WIDE * depth * 2),
        name="qkv",
    )(*pieces, w)


def columns(refs, start):
    return jnp.concatenate([ref[:, start : start + SIZE] for ref in refs], axis=0)


def pack(out, last):
    high = last.astype(bf16).astype(f32)
    mid = (last - high).astype(bf16).astype(f32)
    low = last - high - mid
    out[WIDE:, :] = jnp.concatenate([high, mid, low, jnp.zeros_like(low)], axis=0).astype(bf16)


def unpack(ref):
    tail = ref[WIDE:, :].astype(f32)
    return tail[0:4] + tail[4:8] + tail[8:12]


def state_kernel(a, b, c, d, g, last, out):
    for h in range(HEADS):
        keys = columns((a, b, c, d), WIDE + h * SIZE).astype(f32)
        values = columns((a, b, c, d), 2 * WIDE + h * SIZE)
        scaled = (keys * jnp.exp(last[h : h + 1, 0:1] - g[:, h : h + 1])).astype(bf16)
        state = lax.dot_general(scaled, values, (((0,), (0,)), ((), ())), preferred_element_type=f32)
        out[h * SIZE : (h + 1) * SIZE, :] = state.astype(bf16)
    pack(out, last[...])


def inner_kernel(a, b, c, d, g, gt, row, col, out):
    lower = row[...] >= col[...]
    for h in range(HEADS):
        query = columns((a, b, c, d), h * SIZE)
        keys = columns((a, b, c, d), WIDE + h * SIZE)
        values = columns((a, b, c, d), 2 * WIDE + h * SIZE)
        scores = lax.dot_general(query, keys, (((1,), (1,)), ((), ())), preferred_element_type=f32)
        lagged = g[:, h : h + 1] - gt[h : h + 1, :]
        probs = jnp.where(lower, scores * jnp.exp(jnp.minimum(lagged, 0.0)), 0.0).astype(bf16)
        out[:, h * SIZE : (h + 1) * SIZE] = jnp.dot(probs, values, preferred_element_type=f32)


def row_kernel(at, s0, s1, s2, s3, before, total):
    refs = (s0, s1, s2, s3)
    x = at[0]
    place = [(x - k) & 3 for k in range(N_X)]
    last = [unpack(ref) for ref in refs]

    def between(k, end):
        return sum(jnp.where((place[m] > place[k]) & (place[m] < end), last[m], 0.0) for m in range(N_X))

    reach = [jnp.where(place[k] < x, jnp.exp(between(k, x)), 0.0) for k in range(N_X)]
    whole = [jnp.exp(between(k, N_X)) for k in range(N_X)]
    for h in range(HEADS):
        rows = slice(h * SIZE, (h + 1) * SIZE)
        states = [ref[rows, :].astype(f32) for ref in refs]
        before[rows, :] = sum(states[k] * reach[k][h : h + 1] for k in range(1, N_X))
        total[rows, :] = sum(states[k] * whole[k][h : h + 1] for k in range(N_X)).astype(bf16)
    pack(total, last[0] + last[1] + last[2] + last[3])
    lead = sum(jnp.where(place[k] < x, last[k], 0.0) for k in range(1, N_X))
    before[WIDE:, :] = jnp.concatenate([lead, lead], axis=0)


def normed_kernel(before, t1, t2, t3, a, b, c, d, g, inner, gain, out):
    lead = jnp.exp(before[WIDE : WIDE + HEADS, :])
    r1, r2 = unpack(t1), unpack(t2)
    reach2, reach3 = jnp.exp(r1), jnp.exp(r1 + r2)
    for h in range(HEADS):
        rows = slice(h * SIZE, (h + 1) * SIZE)
        one = slice(h, h + 1)
        earlier = (
            t1[rows, :].astype(f32) + t2[rows, :].astype(f32) * reach2[one] + t3[rows, :].astype(f32) * reach3[one]
        )
        carried = (earlier * lead[one] + before[rows, :]).astype(bf16)
        query = columns((a, b, c, d), h * SIZE).astype(f32)
        scaled = (query * jnp.exp(g[:, one])).astype(bf16)
        mixed = inner[:, rows] + jnp.dot(scaled, carried, preferred_element_type=f32)
        scale = lax.rsqrt(jnp.mean(mixed * mixed, axis=-1, keepdims=True) + norm_eps)
        out[:, rows] = (mixed * scale * gain[:, rows]).astype(bf16)


def whole_call(kernel, args, outs, name, flops, scalars=0):
    nbytes = sum(a.size * a.dtype.itemsize for a in args)
    return pl.pallas_call(
        kernel,
        out_shape=outs,
        in_specs=[pl.BlockSpec(memory_space=pltpu.SMEM)] * scalars
        + [pl.BlockSpec(memory_space=pltpu.VMEM)] * (len(args) - scalars),
        out_specs=jax.tree.map(lambda _: pl.BlockSpec(memory_space=pltpu.VMEM), outs),
        compiler_params=params(),
        cost_estimate=cost(flops, nbytes),
        name=name,
    )(*args)


def project_part(rows, w, outs, m):
    width = w.shape[2]
    part = jnp.dot(rows, w[m], preferred_element_type=f32).astype(bf16)
    for i, out in enumerate(outs):
        out[:, m * width : (m + 1) * width] = part[i * 64 : (i + 1) * 64]


def project_first_kernel(normed, w, own, sib, held, sems):
    per = w.shape[0] // 4
    copies = [
        pltpu.make_async_copy(w.at[pl.ds(i * per, per)], held.at[pl.ds(i * per, per)], sems.at[i]) for i in range(4)
    ]
    for copy in copies:
        copy.start()
    far = normed[FAR : FAR + 128, :]
    for i in range(4):
        copies[i].wait()
        for m in range(i * per, (i + 1) * per):
            project_part(far, held, (own, sib), m)


def project_kernel(blocks, normed, w, *outs):
    rows = jnp.concatenate([normed[64 * b : 64 * b + 64, :] for b in blocks], axis=0)
    for m in range(w.shape[0]):
        project_part(rows, w, outs, m)


def project(normed, w, blocks):
    n_ctx, depth, width = w.shape
    vmem = pl.BlockSpec(memory_space=pltpu.VMEM)
    n = len(blocks)
    return pl.pallas_call(
        functools.partial(project_kernel, blocks),
        out_shape=[jax.ShapeDtypeStruct((64, n_ctx * width), bf16)] * n,
        in_specs=[vmem] * 2,
        out_specs=[vmem] * n,
        compiler_params=params(),
        cost_estimate=cost(2 * 64 * n * depth * n_ctx * width, 2 * depth * n_ctx * width),
        name="project",
    )(normed, w)


def gather_kernel(own, sib, up_plain, down_plain, out):
    mid = up_plain.shape[1]
    for start, other in ((0, down_plain), (mid, up_plain)):
        at = slice(start, start + mid)
        out[:, at] = own[:, at].astype(f32) + sib[:, at].astype(f32) + other[...].astype(f32)


def final_kernel(partial, up_sum, down_sum, out):
    mid = up_sum.shape[1]
    for start, other in ((0, up_sum), (mid, down_sum)):
        at = slice(start, start + mid)
        out[:, at] = (partial[:, at] + other[...].astype(f32)).astype(bf16)


def after(value, *others):
    return lax.optimization_barrier((value, *others))[0]


def plus(*terms):
    total = terms[0].astype(f32)
    for term in terms[1:]:
        total = total + term.astype(f32)
    return total.astype(bf16)


def body(activations, w_qkv, log_decay, gain, w_out):
    tp, ctx = lax.axis_index("tp"), lax.axis_index("ctx")
    y, core = tp // 2, tp % 2
    at = (ctx % N_X).astype(jnp.int32).reshape(1)
    w_all = lax.all_gather(w_out, "ctx", axis=0)

    cumul = jnp.cumsum(log_decay.T, axis=1)
    last = jnp.broadcast_to(cumul[:, -1:], (HEADS, SIZE))
    gt = jnp.roll(cumul.reshape(HEADS, N_Y, 2, 64), -y, axis=1)
    gt = jnp.where(core == 0, gt, gt[:, :, ::-1])
    gt = jnp.concatenate([gt[:, chip, half] for chip, half in PLACES], axis=1)
    g = gt.T
    chip, half = (jnp.array(np.repeat(np.array(p), 64), jnp.int32) for p in zip(*PLACES))
    pos = ((chip + y) & 3) * 128 + ((half + core) & 1) * 64 + jnp.arange(512, dtype=jnp.int32) % 64

    depth = activations.shape[1]
    mid = depth // 2
    low = activations[:, :mid]
    high = after(activations, low)[:, mid:]
    left_low, right_high = to_y(low, 1), to_y(high, -1)
    low_b, high_b = after((low, high), g, gt, last, at, pos)
    left_high, right_low = to_y(high_b, 1), to_y(low_b, -1)
    own2 = to_sibling(activations)
    own2 = after(own2, g, gt, last, at, pos)
    qkv_a, w_qkv = qkv([activations, own2], [(0, 0), (64, 0)], 128, w_qkv, True)
    left_low, right_high = after((left_low, right_high), qkv_a)
    far_low, far_high = to_y(left_low, 1), to_y(right_high, -1)
    low2, high2 = to_sibling(left_low), to_sibling(right_high)
    left_high2, right_low2 = to_sibling(left_high), to_sibling(right_low)
    halves = [(0, 0), (0, mid), (64, 0), (64, mid)]
    near = after((right_low, right_high, left_low, left_high), low2, high2)
    qkv_b = qkv(near, halves, 128, w_qkv)
    far_low, far_high = after((far_low, far_high), qkv_b)
    far_low2, far_high2 = to_sibling(far_low), to_sibling(far_high)
    near2 = after([right_low2, high2, low2, left_high2], far_low, far_high)
    qkv_c = qkv(near2, halves, 128, w_qkv)
    far_low2, far_high2 = after((far_low2, far_high2), qkv_c)
    qkv_d = qkv([far_low, far_high, far_low2, far_high2], halves, 128, w_qkv)
    rows = (qkv_b, qkv_a, qkv_c, qkv_d)

    packed = jax.ShapeDtypeStruct((WIDE + 16, SIZE), bf16)
    state = whole_call(state_kernel, (*rows, g, last), packed, "state", 2 * 512 * WIDE * SIZE)
    row = [state] + [to_x(state, k) for k in range(1, N_X)]
    inner = whole_call(
        inner_kernel,
        (*rows, g, gt, pos.reshape(512, 1), pos.reshape(1, 512)),
        jax.ShapeDtypeStruct((512, WIDE), f32),
        "inner",
        4 * 512 * 512 * WIDE,
    )
    row = after(row, inner)
    before, total = whole_call(
        row_kernel, (at, *row), (jax.ShapeDtypeStruct((WIDE + 8, SIZE), f32), packed), "row", 10 * WIDE * SIZE, 1
    )
    totals = [to_z(total, k) for k in range(1, N_Z)]
    normed = whole_call(
        normed_kernel,
        (before, *totals, *rows, g, inner, gain.reshape(1, WIDE)),
        jax.ShapeDtypeStruct((512, WIDE), bf16),
        "normed",
        2 * 512 * WIDE * SIZE,
    )
    vmem = pl.BlockSpec(memory_space=pltpu.VMEM)
    half = jax.ShapeDtypeStruct((64, depth), bf16)
    far_own, far_sib, w = pl.pallas_call(
        project_first_kernel,
        out_shape=[half, half, pltpu.VMEM(w_all.shape, bf16)],
        in_specs=[vmem, pl.BlockSpec(memory_space=pltpu.HBM)],
        out_specs=[vmem] * 3,
        scratch_shapes=[pltpu.SemaphoreType.DMA((4,))],
        compiler_params=params(),
        cost_estimate=cost(256 * w_all.size, 2 * w_all.size),
        name="project",
    )(normed, pltpu.with_memory_space_constraint(w_all, pltpu.HBM))

    far_sib = to_sibling(far_sib)
    near_parts = project(normed, w, (0, 4, 1, 5))
    far_sib = after(far_sib, near_parts)
    far = plus(far_own[:, :mid], far_sib[:, :mid]), plus(far_own[:, mid:], far_sib[:, mid:])
    from_l, from_r = to_y(far[0], 1), to_y(far[1], -1)
    up_own, up_sib, down_own, down_sib = after(near_parts, *far)
    up_sib, down_sib = to_sibling(up_sib), to_sibling(down_sib)
    up_plain = plus(up_own[:, mid:], up_sib[:, mid:])
    down_plain = plus(down_own[:, :mid], down_sib[:, :mid])
    normed = after(normed, up_plain, down_plain)
    up_plain, down_plain = to_y(up_plain, 1), to_y(down_plain, -1)
    here_own, here_sib = project(normed, w, (2, 3))
    from_l, from_r = after((from_l, from_r), here_own)
    up_sum = to_y(plus(up_own[:, :mid], up_sib[:, :mid], from_l), 1)
    down_sum = to_y(plus(down_own[:, mid:], down_sib[:, mid:], from_r), -1)
    here_sib = to_sibling(here_sib)
    partial = whole_call(
        gather_kernel,
        (here_own, here_sib, up_plain, down_plain),
        jax.ShapeDtypeStruct((64, depth), f32),
        "gather",
        3 * 64 * depth,
    )
    up_sum, down_sum = after((up_sum, down_sum), partial)
    return whole_call(
        final_kernel, (partial, up_sum, down_sum), jax.ShapeDtypeStruct((64, depth), bf16), "final", 64 * depth
    )


def solution(mesh):
    in_specs = (
        P(("ctx", "tp"), None),
        P(None, None, "tp"),
        P("ctx", "tp"),
        P("tp"),
        P("tp", "ctx"),
    )
    out_specs = P(("ctx", "tp"), None)
    return jax.shard_map(body, mesh=mesh, in_specs=in_specs, out_specs=out_specs, check_vma=False)
```

```python
import functools

import jax
import jax.numpy as jnp
import numpy as np
from jax import lax
from jax.experimental import pallas as pl
from jax.experimental.pallas import tpu as pltpu
from jax.sharding import PartitionSpec as P

norm_eps = 1e-06
f32, bf16 = jnp.float32, jnp.bfloat16
HEADS, SIZE = 4, 128
WIDE = HEADS * SIZE
N_X = N_Z = N_Y = 4
FAR = 384
PLACES = ((1, 0), (3, 0), (0, 0), (0, 1), (1, 1), (3, 1), (2, 0), (2, 1))
SHARE = 0.01
VMEM_LIMIT = 20 * 2**20


def params(**kw):
    return pltpu.CompilerParams(vmem_limit_bytes=VMEM_LIMIT, **kw)


def cost(flops, nbytes):
    return pl.CostEstimate(flops=int(flops * SHARE), bytes_accessed=int(nbytes * SHARE), transcendentals=0)


def to_y(a, k):
    return lax.ppermute(a, "tp", [(i, (i // 2 + k) % N_Y * 2 + i % 2) for i in range(2 * N_Y)])


def to_sibling(a):
    return lax.ppermute(a, "tp", [(i, i ^ 1) for i in range(2 * N_Y)])


def to_x(a, k):
    return lax.ppermute(a, "ctx", [(j, j // N_X * N_X + (j + k) % N_X) for j in range(N_X * N_Z)])


def to_z(a, k):
    return lax.ppermute(a, "ctx", [(j, j + N_X * k) for j in range(N_X * N_Z) if j // N_X + k < N_Z])


def place_rows(pieces, layout, rows):
    for piece, (row, col) in zip(pieces, layout):
        rows[row : row + piece.shape[0], col : col + piece.shape[1]] = piece[...]


def activate(member, acc):
    return (acc if member == 2 else acc / (1.0 + jnp.exp(-acc))).astype(bf16)


def qkv_first_kernel(layout, *refs):
    n = len(layout)
    pieces, w, out, held, rows, sems = refs[:n], refs[n], *refs[n + 1 :]
    depth = w.shape[1]
    cut = depth // 4
    copies = [
        [
            pltpu.make_async_copy(w.at[m, pl.ds(k * cut, cut)], held.at[m, pl.ds(k * cut, cut)], sems.at[m, k])
            for k in range(4)
        ]
        for m in range(3)
    ]
    for m in range(3):
        for k in range(4):
            copies[m][k].start()
    place_rows(pieces, layout, rows)
    for m in range(3):
        acc = None
        for k in range(4):
            copies[m][k].wait()
            part = jnp.dot(
                rows[:, k * cut : (k + 1) * cut], held[m, k * cut : (k + 1) * cut], preferred_element_type=f32
            )
            acc = part if acc is None else acc + part
        out[:, m * WIDE : (m + 1) * WIDE] = activate(m, acc)


def qkv_kernel(layout, *refs):
    n = len(layout)
    pieces, w, out, rows = refs[:n], refs[n], refs[n + 1], refs[n + 2]
    place_rows(pieces, layout, rows)
    tile = 256
    for m in range(3):
        for start in range(0, WIDE, tile):
            acc = jnp.dot(rows[...], w[m, :, start : start + tile], preferred_element_type=f32)
            out[:, m * WIDE + start : m * WIDE + start + tile] = activate(m, acc)


def qkv(pieces, layout, count, w, first=False):
    depth = w.shape[1]
    out = jax.ShapeDtypeStruct((count, 3 * WIDE), bf16)
    vmem = pl.BlockSpec(memory_space=pltpu.VMEM)
    return pl.pallas_call(
        functools.partial(qkv_first_kernel if first else qkv_kernel, layout),
        out_shape=(out, pltpu.VMEM(w.shape, bf16)) if first else out,
        in_specs=[vmem] * len(pieces) + [pl.BlockSpec(memory_space=pltpu.HBM) if first else vmem],
        out_specs=(vmem, vmem) if first else vmem,
        scratch_shapes=[pltpu.VMEM((count, depth), bf16)] + ([pltpu.SemaphoreType.DMA((3, 4))] if first else []),
        compiler_params=params(),
        cost_estimate=cost(2 * count * depth * 3 * WIDE, 3 * WIDE * depth * 2),
        name="qkv",
    )(*pieces, w)


def columns(refs, start):
    return jnp.concatenate([ref[:, start : start + SIZE] for ref in refs], axis=0)


def pack(out, last):
    high = last.astype(bf16).astype(f32)
    mid = (last - high).astype(bf16).astype(f32)
    low = last - high - mid
    out[WIDE:, :] = jnp.concatenate([high, mid, low, jnp.zeros_like(low)], axis=0).astype(bf16)


def unpack(ref):
    tail = ref[WIDE:, :].astype(f32)
    return tail[0:4] + tail[4:8] + tail[8:12]


def state_kernel(a, b, c, d, g, last, out):
    for h in range(HEADS):
        keys = columns((a, b, c, d), WIDE + h * SIZE).astype(f32)
        values = columns((a, b, c, d), 2 * WIDE + h * SIZE)
        scaled = (keys * jnp.exp(last[h : h + 1, 0:1] - g[:, h : h + 1])).astype(bf16)
        state = lax.dot_general(scaled, values, (((0,), (0,)), ((), ())), preferred_element_type=f32)
        out[h * SIZE : (h + 1) * SIZE, :] = state.astype(bf16)
    pack(out, last[...])


def inner_kernel(a, b, c, d, g, gt, row, col, out):
    lower = row[...] >= col[...]
    for h in range(HEADS):
        query = columns((a, b, c, d), h * SIZE)
        keys = columns((a, b, c, d), WIDE + h * SIZE)
        values = columns((a, b, c, d), 2 * WIDE + h * SIZE)
        scores = lax.dot_general(query, keys, (((1,), (1,)), ((), ())), preferred_element_type=f32)
        lagged = g[:, h : h + 1] - gt[h : h + 1, :]
        probs = jnp.where(lower, scores * jnp.exp(jnp.minimum(lagged, 0.0)), 0.0).astype(bf16)
        out[:, h * SIZE : (h + 1) * SIZE] = jnp.dot(probs, values, preferred_element_type=f32)


def row_kernel(at, s0, s2, s1, s3, before, total):
    refs = (s0, s1, s2, s3)
    x = at[0]
    place = [(x - k) & 3 for k in range(N_X)]
    last = [unpack(ref) for ref in refs]

    def between(k, end):
        return sum(jnp.where((place[m] > place[k]) & (place[m] < end), last[m], 0.0) for m in range(N_X))

    reach = [jnp.where(place[k] < x, jnp.exp(between(k, x)), 0.0) for k in range(N_X)]
    whole = [jnp.exp(between(k, N_X)) for k in range(N_X)]
    for h in range(HEADS):
        rows = slice(h * SIZE, (h + 1) * SIZE)
        states = [ref[rows, :].astype(f32) for ref in refs]
        before[rows, :] = sum(states[k] * reach[k][h : h + 1] for k in range(1, N_X))
        total[rows, :] = sum(states[k] * whole[k][h : h + 1] for k in range(N_X)).astype(bf16)
    pack(total, last[0] + last[1] + last[2] + last[3])
    lead = sum(jnp.where(place[k] < x, last[k], 0.0) for k in range(1, N_X))
    before[WIDE:, :] = jnp.concatenate([lead, lead], axis=0)


def normed_kernel(before, t2, t1, t3, a, b, c, d, g, inner, gain, out):
    lead = jnp.exp(before[WIDE : WIDE + HEADS, :])
    r1, r2 = unpack(t1), unpack(t2)
    reach2, reach3 = jnp.exp(r1), jnp.exp(r1 + r2)
    for h in range(HEADS):
        rows = slice(h * SIZE, (h + 1) * SIZE)
        one = slice(h, h + 1)
        earlier = (
            t1[rows, :].astype(f32) + t2[rows, :].astype(f32) * reach2[one] + t3[rows, :].astype(f32) * reach3[one]
        )
        carried = (earlier * lead[one] + before[rows, :]).astype(bf16)
        query = columns((a, b, c, d), h * SIZE).astype(f32)
        scaled = (query * jnp.exp(g[:, one])).astype(bf16)
        mixed = inner[:, rows] + jnp.dot(scaled, carried, preferred_element_type=f32)
        scale = lax.rsqrt(jnp.mean(mixed * mixed, axis=-1, keepdims=True) + norm_eps)
        out[:, rows] = (mixed * scale * gain[:, rows]).astype(bf16)


def whole_call(kernel, args, outs, name, flops, scalars=0):
    nbytes = sum(a.size * a.dtype.itemsize for a in args)
    return pl.pallas_call(
        kernel,
        out_shape=outs,
        in_specs=[pl.BlockSpec(memory_space=pltpu.SMEM)] * scalars
        + [pl.BlockSpec(memory_space=pltpu.VMEM)] * (len(args) - scalars),
        out_specs=jax.tree.map(lambda _: pl.BlockSpec(memory_space=pltpu.VMEM), outs),
        compiler_params=params(),
        cost_estimate=cost(flops, nbytes),
        name=name,
    )(*args)


def project_part(rows, w, outs, m):
    width = w.shape[2]
    part = jnp.dot(rows, w[m], preferred_element_type=f32).astype(bf16)
    for i, out in enumerate(outs):
        out[:, m * width : (m + 1) * width] = part[i * 64 : (i + 1) * 64]


def project_first_kernel(normed, w, own, sib, held, sems):
    n = w.shape[0]
    copies = [pltpu.make_async_copy(w.at[m], held.at[m], sems.at[m]) for m in range(n)]
    for copy in copies:
        copy.start()
    far = normed[FAR : FAR + 128, :]
    for m in range(n):
        copies[m].wait()
        project_part(far, held, (own, sib), m)


def project_kernel(blocks, normed, w, *outs):
    rows = jnp.concatenate([normed[64 * b : 64 * b + 64, :] for b in blocks], axis=0)
    for m in range(w.shape[0]):
        project_part(rows, w, outs, m)


def project(normed, w, blocks):
    n_ctx, depth, width = w.shape
    vmem = pl.BlockSpec(memory_space=pltpu.VMEM)
    n = len(blocks)
    return pl.pallas_call(
        functools.partial(project_kernel, blocks),
        out_shape=[jax.ShapeDtypeStruct((64, n_ctx * width), bf16)] * n,
        in_specs=[vmem] * 2,
        out_specs=[vmem] * n,
        compiler_params=params(),
        cost_estimate=cost(2 * 64 * n * depth * n_ctx * width, 2 * depth * n_ctx * width),
        name="project",
    )(normed, w)


def gather_kernel(own, sib, up_plain, down_plain, out):
    mid = up_plain.shape[1]
    for start, other in ((0, down_plain), (mid, up_plain)):
        at = slice(start, start + mid)
        out[:, at] = own[:, at].astype(f32) + sib[:, at].astype(f32) + other[...].astype(f32)


def final_kernel(partial, up_sum, down_sum, out):
    mid = up_sum.shape[1]
    for start, other in ((0, up_sum), (mid, down_sum)):
        at = slice(start, start + mid)
        out[:, at] = (partial[:, at] + other[...].astype(f32)).astype(bf16)


def after(value, *others):
    return lax.optimization_barrier((value, *others))[0]


def plus(*terms):
    total = terms[0].astype(f32)
    for term in terms[1:]:
        total = total + term.astype(f32)
    return total.astype(bf16)


def body(activations, w_qkv, log_decay, gain, w_out):
    tp, ctx = lax.axis_index("tp"), lax.axis_index("ctx")
    y, core = tp // 2, tp % 2
    at = (ctx % N_X).astype(jnp.int32).reshape(1)
    w_all = lax.all_gather(w_out, "ctx", axis=0)

    cumul = jnp.cumsum(log_decay.T, axis=1)
    last = jnp.broadcast_to(cumul[:, -1:], (HEADS, SIZE))
    gt = jnp.roll(cumul.reshape(HEADS, N_Y, 2, 64), -y, axis=1)
    gt = jnp.where(core == 0, gt, gt[:, :, ::-1])
    gt = jnp.concatenate([gt[:, chip, half] for chip, half in PLACES], axis=1)
    g = gt.T
    chip, half = (jnp.array(np.repeat(np.array(p), 64), jnp.int32) for p in zip(*PLACES))
    pos = ((chip + y) & 3) * 128 + ((half + core) & 1) * 64 + jnp.arange(512, dtype=jnp.int32) % 64

    depth = activations.shape[1]
    mid = depth // 2
    low = activations[:, :mid]
    high = after(activations, low)[:, mid:]
    left_low, right_high = to_y(low, 1), to_y(high, -1)
    low_b, high_b = after((low, high), g, gt, last, at, pos)
    left_high, right_low = to_y(high_b, 1), to_y(low_b, -1)
    own2 = to_sibling(activations)
    own2 = after(own2, g, gt, last, at, pos)
    qkv_a, w_qkv = qkv([activations, own2], [(0, 0), (64, 0)], 128, w_qkv, True)
    left_low, right_high = after((left_low, right_high), qkv_a)
    far_low, far_high = to_y(left_low, 1), to_y(right_high, -1)
    low2, high2 = to_sibling(left_low), to_sibling(right_high)
    left_high2, right_low2 = to_sibling(left_high), to_sibling(right_low)
    halves = [(0, 0), (0, mid), (64, 0), (64, mid)]
    near = after((right_low, right_high, left_low, left_high), low2, high2)
    qkv_b = qkv(near, halves, 128, w_qkv)
    far_low, far_high = after((far_low, far_high), qkv_b)
    far_low2, far_high2 = to_sibling(far_low), to_sibling(far_high)
    near2 = after([right_low2, high2, low2, left_high2], far_low, far_high)
    qkv_c = qkv(near2, halves, 128, w_qkv)
    far_low2, far_high2 = after((far_low2, far_high2), qkv_c)
    qkv_d = qkv([far_low, far_high, far_low2, far_high2], halves, 128, w_qkv)
    rows = (qkv_b, qkv_a, qkv_c, qkv_d)

    packed = jax.ShapeDtypeStruct((WIDE + 16, SIZE), bf16)
    state = whole_call(state_kernel, (*rows, g, last), packed, "state", 2 * 512 * WIDE * SIZE)
    row = [state] + [to_x(state, k) for k in (2, 1, 3)]
    inner = whole_call(
        inner_kernel,
        (*rows, g, gt, pos.reshape(512, 1), pos.reshape(1, 512)),
        jax.ShapeDtypeStruct((512, WIDE), f32),
        "inner",
        4 * 512 * 512 * WIDE,
    )
    row = after(row, inner)
    before, total = whole_call(
        row_kernel, (at, *row), (jax.ShapeDtypeStruct((WIDE + 8, SIZE), f32), packed), "row", 10 * WIDE * SIZE, 1
    )
    totals = [to_z(total, k) for k in (2, 1, 3)]
    normed = whole_call(
        normed_kernel,
        (before, *totals, *rows, g, inner, gain.reshape(1, WIDE)),
        jax.ShapeDtypeStruct((512, WIDE), bf16),
        "normed",
        2 * 512 * WIDE * SIZE,
    )
    vmem = pl.BlockSpec(memory_space=pltpu.VMEM)
    half = jax.ShapeDtypeStruct((64, depth), bf16)
    far_own, far_sib, w = pl.pallas_call(
        project_first_kernel,
        out_shape=[half, half, pltpu.VMEM(w_all.shape, bf16)],
        in_specs=[vmem, pl.BlockSpec(memory_space=pltpu.HBM)],
        out_specs=[vmem] * 3,
        scratch_shapes=[pltpu.SemaphoreType.DMA((w_all.shape[0],))],
        compiler_params=params(),
        cost_estimate=cost(256 * w_all.size, 2 * w_all.size),
        name="project",
    )(normed, pltpu.with_memory_space_constraint(w_all, pltpu.HBM))

    far_sib = to_sibling(far_sib)
    near_parts = project(normed, w, (0, 4, 1, 5))
    far_sib = after(far_sib, near_parts)
    far = plus(far_own[:, :mid], far_sib[:, :mid]), plus(far_own[:, mid:], far_sib[:, mid:])
    from_l, from_r = to_y(far[0], 1), to_y(far[1], -1)
    up_own, up_sib, down_own, down_sib = after(near_parts, *far)
    up_sib, down_sib = to_sibling(up_sib), to_sibling(down_sib)
    up_plain = plus(up_own[:, mid:], up_sib[:, mid:])
    down_plain = plus(down_own[:, :mid], down_sib[:, :mid])
    normed = after(normed, up_plain, down_plain)
    up_plain, down_plain = to_y(up_plain, 1), to_y(down_plain, -1)
    here_own, here_sib = project(normed, w, (2, 3))
    from_l, from_r = after((from_l, from_r), here_own)
    up_sum = to_y(plus(up_own[:, :mid], up_sib[:, :mid], from_l), 1)
    down_sum = to_y(plus(down_own[:, mid:], down_sib[:, mid:], from_r), -1)
    here_sib = to_sibling(here_sib)
    partial = whole_call(
        gather_kernel,
        (here_own, here_sib, up_plain, down_plain),
        jax.ShapeDtypeStruct((64, depth), f32),
        "gather",
        3 * 64 * depth,
    )
    up_sum, down_sum = after((up_sum, down_sum), partial)
    return whole_call(
        final_kernel, (partial, up_sum, down_sum), jax.ShapeDtypeStruct((64, depth), bf16), "final", 64 * depth
    )


def solution(mesh):
    in_specs = (
        P(("ctx", "tp"), None),
        P(None, None, "tp"),
        P("ctx", "tp"),
        P("tp"),
        P("tp", "ctx"),
    )
    out_specs = P(("ctx", "tp"), None)
    return jax.shard_map(body, mesh=mesh, in_specs=in_specs, out_specs=out_specs, check_vma=False)
```

```python
import functools

import jax
import jax.numpy as jnp
import numpy as np
from jax import lax
from jax.experimental import pallas as pl
from jax.experimental.pallas import tpu as pltpu
from jax.sharding import PartitionSpec as P

norm_eps = 1e-06
f32, bf16 = jnp.float32, jnp.bfloat16
HEADS, SIZE = 4, 128
WIDE = HEADS * SIZE
N_X = N_Z = N_Y = 4
FAR = 384
PLACES = ((1, 0), (3, 0), (0, 0), (0, 1), (1, 1), (3, 1), (2, 0), (2, 1))
SHARE = 0.01
VMEM_LIMIT = 20 * 2**20


def params(**kw):
    return pltpu.CompilerParams(vmem_limit_bytes=VMEM_LIMIT, **kw)


def cost(flops, nbytes):
    return pl.CostEstimate(flops=int(flops * SHARE), bytes_accessed=int(nbytes * SHARE), transcendentals=0)


def to_y(a, k):
    return lax.ppermute(a, "tp", [(i, (i // 2 + k) % N_Y * 2 + i % 2) for i in range(2 * N_Y)])


def to_sibling(a):
    return lax.ppermute(a, "tp", [(i, i ^ 1) for i in range(2 * N_Y)])


def to_x(a, k):
    return lax.ppermute(a, "ctx", [(j, j // N_X * N_X + (j + k) % N_X) for j in range(N_X * N_Z)])


def to_z(a, k):
    return lax.ppermute(a, "ctx", [(j, j + N_X * k) for j in range(N_X * N_Z) if j // N_X + k < N_Z])


def place_rows(pieces, layout, rows):
    for piece, (row, col) in zip(pieces, layout):
        rows[row : row + piece.shape[0], col : col + piece.shape[1]] = piece[...]


def activate(member, acc):
    return (acc if member == 2 else acc / (1.0 + jnp.exp(-acc))).astype(bf16)


def qkv_first_kernel(layout, *refs):
    n = len(layout)
    pieces, w, out, held, rows, sems = refs[:n], refs[n], *refs[n + 1 :]
    depth = w.shape[1]
    cut = depth // 4
    copies = [
        [
            pltpu.make_async_copy(w.at[m, pl.ds(k * cut, cut)], held.at[m, pl.ds(k * cut, cut)], sems.at[m, k])
            for k in range(4)
        ]
        for m in range(3)
    ]
    for m in range(3):
        for k in range(4):
            copies[m][k].start()
    place_rows(pieces, layout, rows)
    for m in range(3):
        acc = None
        for k in range(4):
            copies[m][k].wait()
            part = jnp.dot(
                rows[:, k * cut : (k + 1) * cut], held[m, k * cut : (k + 1) * cut], preferred_element_type=f32
            )
            acc = part if acc is None else acc + part
        out[:, m * WIDE : (m + 1) * WIDE] = activate(m, acc)


def qkv_kernel(layout, *refs):
    n = len(layout)
    pieces, w, out, rows = refs[:n], refs[n], refs[n + 1], refs[n + 2]
    place_rows(pieces, layout, rows)
    tile = 256
    for m in range(3):
        for start in range(0, WIDE, tile):
            acc = jnp.dot(rows[...], w[m, :, start : start + tile], preferred_element_type=f32)
            out[:, m * WIDE + start : m * WIDE + start + tile] = activate(m, acc)


def qkv(pieces, layout, count, w, first=False):
    depth = w.shape[1]
    out = jax.ShapeDtypeStruct((count, 3 * WIDE), bf16)
    vmem = pl.BlockSpec(memory_space=pltpu.VMEM)
    return pl.pallas_call(
        functools.partial(qkv_first_kernel if first else qkv_kernel, layout),
        out_shape=(out, pltpu.VMEM(w.shape, bf16)) if first else out,
        in_specs=[vmem] * len(pieces) + [pl.BlockSpec(memory_space=pltpu.HBM) if first else vmem],
        out_specs=(vmem, vmem) if first else vmem,
        scratch_shapes=[pltpu.VMEM((count, depth), bf16)] + ([pltpu.SemaphoreType.DMA((3, 4))] if first else []),
        compiler_params=params(),
        cost_estimate=cost(2 * count * depth * 3 * WIDE, 3 * WIDE * depth * 2),
        name="qkv",
    )(*pieces, w)


def columns(refs, start):
    return jnp.concatenate([ref[:, start : start + SIZE] for ref in refs], axis=0)


def pack(out, last):
    high = last.astype(bf16).astype(f32)
    mid = (last - high).astype(bf16).astype(f32)
    low = last - high - mid
    out[WIDE:, :] = jnp.concatenate([high, mid, low, jnp.zeros_like(low)], axis=0).astype(bf16)


def unpack(ref):
    tail = ref[WIDE:, :].astype(f32)
    return tail[0:4] + tail[4:8] + tail[8:12]


def state_kernel(a, b, c, d, g, last, out):
    for h in range(HEADS):
        keys = columns((a, b, c, d), WIDE + h * SIZE).astype(f32)
        values = columns((a, b, c, d), 2 * WIDE + h * SIZE)
        scaled = (keys * jnp.exp(last[h : h + 1, 0:1] - g[:, h : h + 1])).astype(bf16)
        state = lax.dot_general(scaled, values, (((0,), (0,)), ((), ())), preferred_element_type=f32)
        out[h * SIZE : (h + 1) * SIZE, :] = state.astype(bf16)
    pack(out, last[...])


def inner_kernel(a, b, c, d, g, gt, row, col, out):
    lower = row[...] >= col[...]
    for h in range(HEADS):
        query = columns((a, b, c, d), h * SIZE)
        keys = columns((a, b, c, d), WIDE + h * SIZE)
        values = columns((a, b, c, d), 2 * WIDE + h * SIZE)
        scores = lax.dot_general(query, keys, (((1,), (1,)), ((), ())), preferred_element_type=f32)
        lagged = g[:, h : h + 1] - gt[h : h + 1, :]
        probs = jnp.where(lower, scores * jnp.exp(jnp.minimum(lagged, 0.0)), 0.0).astype(bf16)
        out[:, h * SIZE : (h + 1) * SIZE] = jnp.dot(probs, values, preferred_element_type=f32)


def row_kernel(at, s0, s2, s1, s3, before, total):
    refs = (s0, s1, s2, s3)
    x = at[0]
    place = [(x - k) & 3 for k in range(N_X)]
    last = [unpack(ref) for ref in refs]

    def between(k, end):
        return sum(jnp.where((place[m] > place[k]) & (place[m] < end), last[m], 0.0) for m in range(N_X))

    reach = [jnp.where(place[k] < x, jnp.exp(between(k, x)), 0.0) for k in range(N_X)]
    whole = [jnp.exp(between(k, N_X)) for k in range(N_X)]
    for h in range(HEADS):
        rows = slice(h * SIZE, (h + 1) * SIZE)
        states = [ref[rows, :].astype(f32) for ref in refs]
        before[rows, :] = sum(states[k] * reach[k][h : h + 1] for k in range(1, N_X))
        total[rows, :] = sum(states[k] * whole[k][h : h + 1] for k in range(N_X)).astype(bf16)
    pack(total, last[0] + last[1] + last[2] + last[3])
    lead = sum(jnp.where(place[k] < x, last[k], 0.0) for k in range(1, N_X))
    before[WIDE:, :] = jnp.concatenate([lead, lead], axis=0)


def normed_kernel(before, t2, t1, t3, a, b, c, d, g, inner, gain, out):
    lead = jnp.exp(before[WIDE : WIDE + HEADS, :])
    r1, r2 = unpack(t1), unpack(t2)
    reach2, reach3 = jnp.exp(r1), jnp.exp(r1 + r2)
    for h in range(HEADS):
        rows = slice(h * SIZE, (h + 1) * SIZE)
        one = slice(h, h + 1)
        earlier = (
            t1[rows, :].astype(f32) + t2[rows, :].astype(f32) * reach2[one] + t3[rows, :].astype(f32) * reach3[one]
        )
        carried = (earlier * lead[one] + before[rows, :]).astype(bf16)
        query = columns((a, b, c, d), h * SIZE).astype(f32)
        scaled = (query * jnp.exp(g[:, one])).astype(bf16)
        mixed = inner[:, rows] + jnp.dot(scaled, carried, preferred_element_type=f32)
        scale = lax.rsqrt(jnp.mean(mixed * mixed, axis=-1, keepdims=True) + norm_eps)
        out[:, rows] = (mixed * scale * gain[:, rows]).astype(bf16)


def whole_call(kernel, args, outs, name, flops, scalars=0):
    nbytes = sum(a.size * a.dtype.itemsize for a in args)
    return pl.pallas_call(
        kernel,
        out_shape=outs,
        in_specs=[pl.BlockSpec(memory_space=pltpu.SMEM)] * scalars
        + [pl.BlockSpec(memory_space=pltpu.VMEM)] * (len(args) - scalars),
        out_specs=jax.tree.map(lambda _: pl.BlockSpec(memory_space=pltpu.VMEM), outs),
        compiler_params=params(),
        cost_estimate=cost(flops, nbytes),
        name=name,
    )(*args)


def project_part(rows, w, outs, m):
    width = w.shape[2]
    part = jnp.dot(rows, w[m], preferred_element_type=f32).astype(bf16)
    for i, out in enumerate(outs):
        out[:, m * width : (m + 1) * width] = part[i * 64 : (i + 1) * 64]


def project_first_kernel(normed, w, own, sib, held, sems):
    per = w.shape[0] // 4
    copies = [
        pltpu.make_async_copy(w.at[pl.ds(i * per, per)], held.at[pl.ds(i * per, per)], sems.at[i]) for i in range(4)
    ]
    for copy in copies:
        copy.start()
    far = normed[FAR : FAR + 128, :]
    for i in range(4):
        copies[i].wait()
        for m in range(i * per, (i + 1) * per):
            project_part(far, held, (own, sib), m)


def project_kernel(blocks, normed, w, *outs):
    rows = jnp.concatenate([normed[64 * b : 64 * b + 64, :] for b in blocks], axis=0)
    for m in range(w.shape[0]):
        project_part(rows, w, outs, m)


def project(normed, w, blocks):
    n_ctx, depth, width = w.shape
    vmem = pl.BlockSpec(memory_space=pltpu.VMEM)
    n = len(blocks)
    return pl.pallas_call(
        functools.partial(project_kernel, blocks),
        out_shape=[jax.ShapeDtypeStruct((64, n_ctx * width), bf16)] * n,
        in_specs=[vmem] * 2,
        out_specs=[vmem] * n,
        compiler_params=params(),
        cost_estimate=cost(2 * 64 * n * depth * n_ctx * width, 2 * depth * n_ctx * width),
        name="project",
    )(normed, w)


def gather_kernel(own, sib, up_plain, down_plain, out):
    mid = up_plain.shape[1]
    for start, other in ((0, down_plain), (mid, up_plain)):
        at = slice(start, start + mid)
        out[:, at] = own[:, at].astype(f32) + sib[:, at].astype(f32) + other[...].astype(f32)


def final_kernel(partial, up_sum, down_sum, out):
    mid = up_sum.shape[1]
    for start, other in ((0, up_sum), (mid, down_sum)):
        at = slice(start, start + mid)
        out[:, at] = (partial[:, at] + other[...].astype(f32)).astype(bf16)


def after(value, *others):
    return lax.optimization_barrier((value, *others))[0]


def plus(*terms):
    total = terms[0].astype(f32)
    for term in terms[1:]:
        total = total + term.astype(f32)
    return total.astype(bf16)


def body(activations, w_qkv, log_decay, gain, w_out):
    tp, ctx = lax.axis_index("tp"), lax.axis_index("ctx")
    y, core = tp // 2, tp % 2
    at = (ctx % N_X).astype(jnp.int32).reshape(1)
    w_all = lax.all_gather(w_out, "ctx", axis=0)

    cumul = jnp.cumsum(log_decay.T, axis=1)
    last = jnp.broadcast_to(cumul[:, -1:], (HEADS, SIZE))
    gt = jnp.roll(cumul.reshape(HEADS, N_Y, 2, 64), -y, axis=1)
    gt = jnp.where(core == 0, gt, gt[:, :, ::-1])
    gt = jnp.concatenate([gt[:, chip, half] for chip, half in PLACES], axis=1)
    g = gt.T
    chip, half = (jnp.array(np.repeat(np.array(p), 64), jnp.int32) for p in zip(*PLACES))
    pos = ((chip + y) & 3) * 128 + ((half + core) & 1) * 64 + jnp.arange(512, dtype=jnp.int32) % 64

    depth = activations.shape[1]
    mid = depth // 2
    low = activations[:, :mid]
    high = after(activations, low)[:, mid:]
    left_low, right_high = to_y(low, 1), to_y(high, -1)
    low_b, high_b = after((low, high), g, gt, last, at, pos)
    left_high, right_low = to_y(high_b, 1), to_y(low_b, -1)
    own2 = to_sibling(activations)
    own2 = after(own2, g, gt, last, at, pos)
    qkv_a, w_qkv = qkv([activations, own2], [(0, 0), (64, 0)], 128, w_qkv, True)
    left_low, right_high = after((left_low, right_high), qkv_a)
    far_low, far_high = to_y(left_low, 1), to_y(right_high, -1)
    low2, high2 = to_sibling(left_low), to_sibling(right_high)
    left_high2, right_low2 = to_sibling(left_high), to_sibling(right_low)
    halves = [(0, 0), (0, mid), (64, 0), (64, mid)]
    near = after((right_low, right_high, left_low, left_high), low2, high2)
    qkv_b = qkv(near, halves, 128, w_qkv)
    far_low, far_high = after((far_low, far_high), qkv_b)
    far_low2, far_high2 = to_sibling(far_low), to_sibling(far_high)
    near2 = after([right_low2, high2, low2, left_high2], far_low, far_high)
    qkv_c = qkv(near2, halves, 128, w_qkv)
    far_low2, far_high2 = after((far_low2, far_high2), qkv_c)
    qkv_d = qkv([far_low, far_high, far_low2, far_high2], halves, 128, w_qkv)
    rows = (qkv_b, qkv_a, qkv_c, qkv_d)

    packed = jax.ShapeDtypeStruct((WIDE + 16, SIZE), bf16)
    state = whole_call(state_kernel, (*rows, g, last), packed, "state", 2 * 512 * WIDE * SIZE)
    row = [state] + [to_x(state, k) for k in (2, 1, 3)]
    inner = whole_call(
        inner_kernel,
        (*rows, g, gt, pos.reshape(512, 1), pos.reshape(1, 512)),
        jax.ShapeDtypeStruct((512, WIDE), f32),
        "inner",
        4 * 512 * 512 * WIDE,
    )
    row = after(row, inner)
    before, total = whole_call(
        row_kernel, (at, *row), (jax.ShapeDtypeStruct((WIDE + 8, SIZE), f32), packed), "row", 10 * WIDE * SIZE, 1
    )
    totals = [to_z(total, k) for k in (2, 1, 3)]
    normed = whole_call(
        normed_kernel,
        (before, *totals, *rows, g, inner, gain.reshape(1, WIDE)),
        jax.ShapeDtypeStruct((512, WIDE), bf16),
        "normed",
        2 * 512 * WIDE * SIZE,
    )
    vmem = pl.BlockSpec(memory_space=pltpu.VMEM)
    half = jax.ShapeDtypeStruct((64, depth), bf16)
    far_own, far_sib, w = pl.pallas_call(
        project_first_kernel,
        out_shape=[half, half, pltpu.VMEM(w_all.shape, bf16)],
        in_specs=[vmem, pl.BlockSpec(memory_space=pltpu.HBM)],
        out_specs=[vmem] * 3,
        scratch_shapes=[pltpu.SemaphoreType.DMA((4,))],
        compiler_params=params(),
        cost_estimate=cost(256 * w_all.size, 2 * w_all.size),
        name="project",
    )(normed, pltpu.with_memory_space_constraint(w_all, pltpu.HBM))

    far_sib = to_sibling(far_sib)
    near_parts = project(normed, w, (0, 4, 1, 5))
    far_sib = after(far_sib, near_parts)
    far = plus(far_own[:, :mid], far_sib[:, :mid]), plus(far_own[:, mid:], far_sib[:, mid:])
    from_l, from_r = to_y(far[0], 1), to_y(far[1], -1)
    up_own, up_sib, down_own, down_sib = after(near_parts, *far)
    up_sib, down_sib = to_sibling(up_sib), to_sibling(down_sib)
    up_plain = plus(up_own[:, mid:], up_sib[:, mid:])
    down_plain = plus(down_own[:, :mid], down_sib[:, :mid])
    normed = after(normed, up_plain, down_plain)
    up_plain, down_plain = to_y(up_plain, 1), to_y(down_plain, -1)
    here_own, here_sib = project(normed, w, (2, 3))
    from_l, from_r = after((from_l, from_r), here_own)
    up_sum = to_y(plus(up_own[:, :mid], up_sib[:, :mid], from_l), 1)
    down_sum = to_y(plus(down_own[:, mid:], down_sib[:, mid:], from_r), -1)
    here_sib = to_sibling(here_sib)
    partial = whole_call(
        gather_kernel,
        (here_own, here_sib, up_plain, down_plain),
        jax.ShapeDtypeStruct((64, depth), f32),
        "gather",
        3 * 64 * depth,
    )
    up_sum, down_sum = after((up_sum, down_sum), partial)
    return whole_call(
        final_kernel, (partial, up_sum, down_sum), jax.ShapeDtypeStruct((64, depth), bf16), "final", 64 * depth
    )


def solution(mesh):
    in_specs = (
        P(("ctx", "tp"), None),
        P(None, None, "tp"),
        P("ctx", "tp"),
        P("tp"),
        P("tp", "ctx"),
    )
    out_specs = P(("ctx", "tp"), None)
    return jax.shard_map(body, mesh=mesh, in_specs=in_specs, out_specs=out_specs, check_vma=False)
```

```python
import functools

import jax
import jax.numpy as jnp
import numpy as np
from jax import lax
from jax.experimental import pallas as pl
from jax.experimental.pallas import tpu as pltpu
from jax.sharding import PartitionSpec as P

norm_eps = 1e-06
f32, bf16 = jnp.float32, jnp.bfloat16
HEADS, SIZE = 4, 128
WIDE = HEADS * SIZE
N_X = N_Z = N_Y = 4
FAR = 384
PLACES = ((1, 0), (3, 0), (0, 0), (0, 1), (1, 1), (3, 1), (2, 0), (2, 1))
SHARE = 0.01
VMEM_LIMIT = 20 * 2**20


def params(**kw):
    return pltpu.CompilerParams(vmem_limit_bytes=VMEM_LIMIT, **kw)


def cost(flops, nbytes):
    return pl.CostEstimate(flops=int(flops * SHARE), bytes_accessed=int(nbytes * SHARE), transcendentals=0)


def to_y(a, k):
    return lax.ppermute(a, "tp", [(i, (i // 2 + k) % N_Y * 2 + i % 2) for i in range(2 * N_Y)])


def to_sibling(a):
    return lax.ppermute(a, "tp", [(i, i ^ 1) for i in range(2 * N_Y)])


def to_x(a, k):
    return lax.ppermute(a, "ctx", [(j, j // N_X * N_X + (j + k) % N_X) for j in range(N_X * N_Z)])


def to_z(a, k):
    return lax.ppermute(a, "ctx", [(j, j + N_X * k) for j in range(N_X * N_Z) if j // N_X + k < N_Z])


def place_rows(pieces, layout, rows):
    for piece, (row, col) in zip(pieces, layout):
        rows[row : row + piece.shape[0], col : col + piece.shape[1]] = piece[...]


def activate(member, acc):
    return (acc if member == 2 else acc / (1.0 + jnp.exp(-acc))).astype(bf16)


def qkv_first_kernel(layout, *refs):
    n = len(layout)
    pieces, w, out, held, rows, sems = refs[:n], refs[n], *refs[n + 1 :]
    depth = w.shape[1]
    cut = depth // 4
    copies = [
        [
            pltpu.make_async_copy(w.at[m, pl.ds(k * cut, cut)], held.at[m, pl.ds(k * cut, cut)], sems.at[m, k])
            for k in range(4)
        ]
        for m in range(3)
    ]
    for m in range(3):
        for k in range(4):
            copies[m][k].start()
    place_rows(pieces, layout, rows)
    for m in range(3):
        acc = None
        for k in range(4):
            copies[m][k].wait()
            part = jnp.dot(
                rows[:, k * cut : (k + 1) * cut], held[m, k * cut : (k + 1) * cut], preferred_element_type=f32
            )
            acc = part if acc is None else acc + part
        out[:, m * WIDE : (m + 1) * WIDE] = activate(m, acc)


def qkv_kernel(layout, *refs):
    n = len(layout)
    pieces, w, out, rows = refs[:n], refs[n], refs[n + 1], refs[n + 2]
    place_rows(pieces, layout, rows)
    tile = 256
    for m in range(3):
        for start in range(0, WIDE, tile):
            acc = jnp.dot(rows[...], w[m, :, start : start + tile], preferred_element_type=f32)
            out[:, m * WIDE + start : m * WIDE + start + tile] = activate(m, acc)


def qkv(pieces, layout, count, w, first=False):
    depth = w.shape[1]
    out = jax.ShapeDtypeStruct((count, 3 * WIDE), bf16)
    vmem = pl.BlockSpec(memory_space=pltpu.VMEM)
    return pl.pallas_call(
        functools.partial(qkv_first_kernel if first else qkv_kernel, layout),
        out_shape=(out, pltpu.VMEM(w.shape, bf16)) if first else out,
        in_specs=[vmem] * len(pieces) + [pl.BlockSpec(memory_space=pltpu.HBM) if first else vmem],
        out_specs=(vmem, vmem) if first else vmem,
        scratch_shapes=[pltpu.VMEM((count, depth), bf16)] + ([pltpu.SemaphoreType.DMA((3, 4))] if first else []),
        compiler_params=params(),
        cost_estimate=cost(2 * count * depth * 3 * WIDE, 3 * WIDE * depth * 2),
        name="qkv",
    )(*pieces, w)


def columns(refs, start):
    return jnp.concatenate([ref[:, start : start + SIZE] for ref in refs], axis=0)


def pack(out, last):
    high = last.astype(bf16).astype(f32)
    mid = (last - high).astype(bf16).astype(f32)
    low = last - high - mid
    out[WIDE:, :] = jnp.concatenate([high, mid, low, jnp.zeros_like(low)], axis=0).astype(bf16)


def unpack(ref):
    tail = ref[WIDE:, :].astype(f32)
    return tail[0:4] + tail[4:8] + tail[8:12]


def state_kernel(a, b, c, d, g, last, out):
    for h in range(HEADS):
        keys = columns((a, b, c, d), WIDE + h * SIZE).astype(f32)
        values = columns((a, b, c, d), 2 * WIDE + h * SIZE)
        scaled = (keys * jnp.exp(last[h : h + 1, 0:1] - g[:, h : h + 1])).astype(bf16)
        state = lax.dot_general(scaled, values, (((0,), (0,)), ((), ())), preferred_element_type=f32)
        out[h * SIZE : (h + 1) * SIZE, :] = state.astype(bf16)
    pack(out, last[...])


def inner_kernel(a, b, c, d, g, gt, row, col, out):
    lower = row[...] >= col[...]
    for h in range(HEADS):
        query = columns((a, b, c, d), h * SIZE)
        keys = columns((a, b, c, d), WIDE + h * SIZE)
        values = columns((a, b, c, d), 2 * WIDE + h * SIZE)
        scores = lax.dot_general(query, keys, (((1,), (1,)), ((), ())), preferred_element_type=f32)
        lagged = g[:, h : h + 1] - gt[h : h + 1, :]
        probs = jnp.where(lower, scores * jnp.exp(jnp.minimum(lagged, 0.0)), 0.0).astype(bf16)
        out[:, h * SIZE : (h + 1) * SIZE] = jnp.dot(probs, values, preferred_element_type=f32)


def row_kernel(at, s0, s2, s1, s3, before, total):
    refs = (s0, s1, s2, s3)
    x = at[0]
    place = [(x - k) & 3 for k in range(N_X)]
    last = [unpack(ref) for ref in refs]

    def between(k, end):
        return sum(jnp.where((place[m] > place[k]) & (place[m] < end), last[m], 0.0) for m in range(N_X))

    reach = [jnp.where(place[k] < x, jnp.exp(between(k, x)), 0.0) for k in range(N_X)]
    whole = [jnp.exp(between(k, N_X)) for k in range(N_X)]
    for h in range(HEADS):
        rows = slice(h * SIZE, (h + 1) * SIZE)
        states = [ref[rows, :].astype(f32) for ref in refs]
        before[rows, :] = sum(states[k] * reach[k][h : h + 1] for k in range(1, N_X))
        total[rows, :] = sum(states[k] * whole[k][h : h + 1] for k in range(N_X)).astype(bf16)
    pack(total, last[0] + last[1] + last[2] + last[3])
    lead = sum(jnp.where(place[k] < x, last[k], 0.0) for k in range(1, N_X))
    before[WIDE:, :] = jnp.concatenate([lead, lead], axis=0)


def normed_kernel(before, t2, t1, t3, a, b, c, d, g, inner, gain, out):
    lead = jnp.exp(before[WIDE : WIDE + HEADS, :])
    r1, r2 = unpack(t1), unpack(t2)
    reach2, reach3 = jnp.exp(r1), jnp.exp(r1 + r2)
    for h in range(HEADS):
        rows = slice(h * SIZE, (h + 1) * SIZE)
        one = slice(h, h + 1)
        earlier = (
            t1[rows, :].astype(f32) + t2[rows, :].astype(f32) * reach2[one] + t3[rows, :].astype(f32) * reach3[one]
        )
        carried = (earlier * lead[one] + before[rows, :]).astype(bf16)
        query = columns((a, b, c, d), h * SIZE).astype(f32)
        scaled = (query * jnp.exp(g[:, one])).astype(bf16)
        mixed = inner[:, rows] + jnp.dot(scaled, carried, preferred_element_type=f32)
        scale = lax.rsqrt(jnp.mean(mixed * mixed, axis=-1, keepdims=True) + norm_eps)
        out[:, rows] = (mixed * scale * gain[:, rows]).astype(bf16)


def whole_call(kernel, args, outs, name, flops, scalars=0):
    nbytes = sum(a.size * a.dtype.itemsize for a in args)
    return pl.pallas_call(
        kernel,
        out_shape=outs,
        in_specs=[pl.BlockSpec(memory_space=pltpu.SMEM)] * scalars
        + [pl.BlockSpec(memory_space=pltpu.VMEM)] * (len(args) - scalars),
        out_specs=jax.tree.map(lambda _: pl.BlockSpec(memory_space=pltpu.VMEM), outs),
        compiler_params=params(),
        cost_estimate=cost(flops, nbytes),
        name=name,
    )(*args)


def project_part(rows, w, outs, m):
    width = w.shape[2]
    part = jnp.dot(rows, w[m], preferred_element_type=f32).astype(bf16)
    for i, out in enumerate(outs):
        out[:, m * width : (m + 1) * width] = part[i * 64 : (i + 1) * 64]


def project_first_kernel(normed, w, own, sib, held, sems):
    per = w.shape[0] // 2
    copies = [
        pltpu.make_async_copy(w.at[pl.ds(i * per, per)], held.at[pl.ds(i * per, per)], sems.at[i]) for i in range(2)
    ]
    for copy in copies:
        copy.start()
    far = normed[FAR : FAR + 128, :]
    for i in range(2):
        copies[i].wait()
        for m in range(i * per, (i + 1) * per):
            project_part(far, held, (own, sib), m)


def project_kernel(blocks, normed, w, *outs):
    rows = jnp.concatenate([normed[64 * b : 64 * b + 64, :] for b in blocks], axis=0)
    for m in range(w.shape[0]):
        project_part(rows, w, outs, m)


def project(normed, w, blocks):
    n_ctx, depth, width = w.shape
    vmem = pl.BlockSpec(memory_space=pltpu.VMEM)
    n = len(blocks)
    return pl.pallas_call(
        functools.partial(project_kernel, blocks),
        out_shape=[jax.ShapeDtypeStruct((64, n_ctx * width), bf16)] * n,
        in_specs=[vmem] * 2,
        out_specs=[vmem] * n,
        compiler_params=params(),
        cost_estimate=cost(2 * 64 * n * depth * n_ctx * width, 2 * depth * n_ctx * width),
        name="project",
    )(normed, w)


def gather_kernel(own, sib, up_plain, down_plain, out):
    mid = up_plain.shape[1]
    for start, other in ((0, down_plain), (mid, up_plain)):
        at = slice(start, start + mid)
        out[:, at] = own[:, at].astype(f32) + sib[:, at].astype(f32) + other[...].astype(f32)


def final_kernel(partial, up_sum, down_sum, out):
    mid = up_sum.shape[1]
    for start, other in ((0, up_sum), (mid, down_sum)):
        at = slice(start, start + mid)
        out[:, at] = (partial[:, at] + other[...].astype(f32)).astype(bf16)


def after(value, *others):
    return lax.optimization_barrier((value, *others))[0]


def plus(*terms):
    total = terms[0].astype(f32)
    for term in terms[1:]:
        total = total + term.astype(f32)
    return total.astype(bf16)


def body(activations, w_qkv, log_decay, gain, w_out):
    tp, ctx = lax.axis_index("tp"), lax.axis_index("ctx")
    y, core = tp // 2, tp % 2
    at = (ctx % N_X).astype(jnp.int32).reshape(1)
    w_all = lax.all_gather(w_out, "ctx", axis=0)

    cumul = jnp.cumsum(log_decay.T, axis=1)
    last = jnp.broadcast_to(cumul[:, -1:], (HEADS, SIZE))
    gt = jnp.roll(cumul.reshape(HEADS, N_Y, 2, 64), -y, axis=1)
    gt = jnp.where(core == 0, gt, gt[:, :, ::-1])
    gt = jnp.concatenate([gt[:, chip, half] for chip, half in PLACES], axis=1)
    g = gt.T
    chip, half = (jnp.array(np.repeat(np.array(p), 64), jnp.int32) for p in zip(*PLACES))
    pos = ((chip + y) & 3) * 128 + ((half + core) & 1) * 64 + jnp.arange(512, dtype=jnp.int32) % 64

    depth = activations.shape[1]
    mid = depth // 2
    low = activations[:, :mid]
    high = after(activations, low)[:, mid:]
    left_low, right_high = to_y(low, 1), to_y(high, -1)
    low_b, high_b = after((low, high), g, gt, last, at, pos)
    left_high, right_low = to_y(high_b, 1), to_y(low_b, -1)
    own2 = to_sibling(activations)
    own2 = after(own2, g, gt, last, at, pos)
    qkv_a, w_qkv = qkv([activations, own2], [(0, 0), (64, 0)], 128, w_qkv, True)
    left_low, right_high = after((left_low, right_high), qkv_a)
    far_low, far_high = to_y(left_low, 1), to_y(right_high, -1)
    low2, high2 = to_sibling(left_low), to_sibling(right_high)
    left_high2, right_low2 = to_sibling(left_high), to_sibling(right_low)
    halves = [(0, 0), (0, mid), (64, 0), (64, mid)]
    near = after((right_low, right_high, left_low, left_high), low2, high2)
    qkv_b = qkv(near, halves, 128, w_qkv)
    far_low, far_high = after((far_low, far_high), qkv_b)
    far_low2, far_high2 = to_sibling(far_low), to_sibling(far_high)
    near2 = after([right_low2, high2, low2, left_high2], far_low, far_high)
    qkv_c = qkv(near2, halves, 128, w_qkv)
    far_low2, far_high2 = after((far_low2, far_high2), qkv_c)
    qkv_d = qkv([far_low, far_high, far_low2, far_high2], halves, 128, w_qkv)
    rows = (qkv_b, qkv_a, qkv_c, qkv_d)

    packed = jax.ShapeDtypeStruct((WIDE + 16, SIZE), bf16)
    state = whole_call(state_kernel, (*rows, g, last), packed, "state", 2 * 512 * WIDE * SIZE)
    row = [state] + [to_x(state, k) for k in (2, 1, 3)]
    inner = whole_call(
        inner_kernel,
        (*rows, g, gt, pos.reshape(512, 1), pos.reshape(1, 512)),
        jax.ShapeDtypeStruct((512, WIDE), f32),
        "inner",
        4 * 512 * 512 * WIDE,
    )
    row = after(row, inner)
    before, total = whole_call(
        row_kernel, (at, *row), (jax.ShapeDtypeStruct((WIDE + 8, SIZE), f32), packed), "row", 10 * WIDE * SIZE, 1
    )
    totals = [to_z(total, k) for k in (2, 1, 3)]
    normed = whole_call(
        normed_kernel,
        (before, *totals, *rows, g, inner, gain.reshape(1, WIDE)),
        jax.ShapeDtypeStruct((512, WIDE), bf16),
        "normed",
        2 * 512 * WIDE * SIZE,
    )
    vmem = pl.BlockSpec(memory_space=pltpu.VMEM)
    half = jax.ShapeDtypeStruct((64, depth), bf16)
    far_own, far_sib, w = pl.pallas_call(
        project_first_kernel,
        out_shape=[half, half, pltpu.VMEM(w_all.shape, bf16)],
        in_specs=[vmem, pl.BlockSpec(memory_space=pltpu.HBM)],
        out_specs=[vmem] * 3,
        scratch_shapes=[pltpu.SemaphoreType.DMA((2,))],
        compiler_params=params(),
        cost_estimate=cost(256 * w_all.size, 2 * w_all.size),
        name="project",
    )(normed, pltpu.with_memory_space_constraint(w_all, pltpu.HBM))

    far_sib = to_sibling(far_sib)
    near_parts = project(normed, w, (0, 4, 1, 5))
    far_sib = after(far_sib, near_parts)
    far = plus(far_own[:, :mid], far_sib[:, :mid]), plus(far_own[:, mid:], far_sib[:, mid:])
    from_l, from_r = to_y(far[0], 1), to_y(far[1], -1)
    up_own, up_sib, down_own, down_sib = after(near_parts, *far)
    up_sib, down_sib = to_sibling(up_sib), to_sibling(down_sib)
    up_plain = plus(up_own[:, mid:], up_sib[:, mid:])
    down_plain = plus(down_own[:, :mid], down_sib[:, :mid])
    normed = after(normed, up_plain, down_plain)
    up_plain, down_plain = to_y(up_plain, 1), to_y(down_plain, -1)
    here_own, here_sib = project(normed, w, (2, 3))
    from_l, from_r = after((from_l, from_r), here_own)
    up_sum = to_y(plus(up_own[:, :mid], up_sib[:, :mid], from_l), 1)
    down_sum = to_y(plus(down_own[:, mid:], down_sib[:, mid:], from_r), -1)
    here_sib = to_sibling(here_sib)
    partial = whole_call(
        gather_kernel,
        (here_own, here_sib, up_plain, down_plain),
        jax.ShapeDtypeStruct((64, depth), f32),
        "gather",
        3 * 64 * depth,
    )
    up_sum, down_sum = after((up_sum, down_sum), partial)
    return whole_call(
        final_kernel, (partial, up_sum, down_sum), jax.ShapeDtypeStruct((64, depth), bf16), "final", 64 * depth
    )


def solution(mesh):
    in_specs = (
        P(("ctx", "tp"), None),
        P(None, None, "tp"),
        P("ctx", "tp"),
        P("tp"),
        P("tp", "ctx"),
    )
    out_specs = P(("ctx", "tp"), None)
    return jax.shard_map(body, mesh=mesh, in_specs=in_specs, out_specs=out_specs, check_vma=False)
```

```python
import functools

import jax
import jax.numpy as jnp
import numpy as np
from jax import lax
from jax.experimental import pallas as pl
from jax.experimental.pallas import tpu as pltpu
from jax.sharding import PartitionSpec as P

norm_eps = 1e-06
f32, bf16 = jnp.float32, jnp.bfloat16
HEADS, SIZE = 4, 128
WIDE = HEADS * SIZE
N_X = N_Z = N_Y = 4
FAR = 384
PLACES = ((1, 0), (3, 0), (0, 0), (0, 1), (1, 1), (3, 1), (2, 0), (2, 1))
SHARE = 0.01
VMEM_LIMIT = 20 * 2**20


def params(**kw):
    return pltpu.CompilerParams(vmem_limit_bytes=VMEM_LIMIT, **kw)


def cost(flops, nbytes):
    return pl.CostEstimate(flops=int(flops * SHARE), bytes_accessed=int(nbytes * SHARE), transcendentals=0)


def to_y(a, k):
    return lax.ppermute(a, "tp", [(i, (i // 2 + k) % N_Y * 2 + i % 2) for i in range(2 * N_Y)])


def to_sibling(a):
    return lax.ppermute(a, "tp", [(i, i ^ 1) for i in range(2 * N_Y)])


def to_x(a, k):
    return lax.ppermute(a, "ctx", [(j, j // N_X * N_X + (j + k) % N_X) for j in range(N_X * N_Z)])


def to_z(a, k):
    return lax.ppermute(a, "ctx", [(j, j + N_X * k) for j in range(N_X * N_Z) if j // N_X + k < N_Z])


def place_rows(pieces, layout, rows):
    for piece, (row, col) in zip(pieces, layout):
        rows[row : row + piece.shape[0], col : col + piece.shape[1]] = piece[...]


def activate(member, acc):
    return (acc if member == 2 else acc / (1.0 + jnp.exp(-acc))).astype(bf16)


def qkv_first_kernel(layout, *refs):
    n = len(layout)
    pieces, w, out, held, rows, sems = refs[:n], refs[n], *refs[n + 1 :]
    depth = w.shape[1]
    cut = depth // 4
    copies = [
        [
            pltpu.make_async_copy(w.at[m, pl.ds(k * cut, cut)], held.at[m, pl.ds(k * cut, cut)], sems.at[m, k])
            for k in range(4)
        ]
        for m in range(3)
    ]
    for m in range(3):
        for k in range(4):
            copies[m][k].start()
    place_rows(pieces, layout, rows)
    for m in range(3):
        acc = None
        for k in range(4):
            copies[m][k].wait()
            part = jnp.dot(
                rows[:, k * cut : (k + 1) * cut], held[m, k * cut : (k + 1) * cut], preferred_element_type=f32
            )
            acc = part if acc is None else acc + part
        out[:, m * WIDE : (m + 1) * WIDE] = activate(m, acc)


def qkv_kernel(layout, *refs):
    n = len(layout)
    pieces, w, out, rows = refs[:n], refs[n], refs[n + 1], refs[n + 2]
    place_rows(pieces, layout, rows)
    tile = 256
    for m in range(3):
        for start in range(0, WIDE, tile):
            acc = jnp.dot(rows[...], w[m, :, start : start + tile], preferred_element_type=f32)
            out[:, m * WIDE + start : m * WIDE + start + tile] = activate(m, acc)


def qkv(pieces, layout, count, w, first=False):
    depth = w.shape[1]
    out = jax.ShapeDtypeStruct((count, 3 * WIDE), bf16)
    vmem = pl.BlockSpec(memory_space=pltpu.VMEM)
    return pl.pallas_call(
        functools.partial(qkv_first_kernel if first else qkv_kernel, layout),
        out_shape=(out, pltpu.VMEM(w.shape, bf16)) if first else out,
        in_specs=[vmem] * len(pieces) + [pl.BlockSpec(memory_space=pltpu.HBM) if first else vmem],
        out_specs=(vmem, vmem) if first else vmem,
        scratch_shapes=[pltpu.VMEM((count, depth), bf16)] + ([pltpu.SemaphoreType.DMA((3, 4))] if first else []),
        compiler_params=params(),
        cost_estimate=cost(2 * count * depth * 3 * WIDE, 3 * WIDE * depth * 2),
        name="qkv",
    )(*pieces, w)


def columns(refs, start):
    return jnp.concatenate([ref[:, start : start + SIZE] for ref in refs], axis=0)


def pack(out, last):
    high = last.astype(bf16).astype(f32)
    mid = (last - high).astype(bf16).astype(f32)
    low = last - high - mid
    out[WIDE:, :] = jnp.concatenate([high, mid, low, jnp.zeros_like(low)], axis=0).astype(bf16)


def unpack(ref):
    tail = ref[WIDE:, :].astype(f32)
    return tail[0:4] + tail[4:8] + tail[8:12]


def state_kernel(a, b, c, d, g, last, out):
    for h in range(HEADS):
        keys = columns((a, b, c, d), WIDE + h * SIZE).astype(f32)
        values = columns((a, b, c, d), 2 * WIDE + h * SIZE)
        scaled = (keys * jnp.exp(last[h : h + 1, 0:1] - g[:, h : h + 1])).astype(bf16)
        state = lax.dot_general(scaled, values, (((0,), (0,)), ((), ())), preferred_element_type=f32)
        out[h * SIZE : (h + 1) * SIZE, :] = state.astype(bf16)
    pack(out, last[...])


def inner_kernel(a, b, c, d, g, gt, row, col, out):
    lower = row[...] >= col[...]
    for h in range(HEADS):
        query = columns((a, b, c, d), h * SIZE)
        keys = columns((a, b, c, d), WIDE + h * SIZE)
        values = columns((a, b, c, d), 2 * WIDE + h * SIZE)
        scores = lax.dot_general(query, keys, (((1,), (1,)), ((), ())), preferred_element_type=f32)
        lagged = g[:, h : h + 1] - gt[h : h + 1, :]
        probs = jnp.where(lower, scores * jnp.exp(jnp.minimum(lagged, 0.0)), 0.0).astype(bf16)
        out[:, h * SIZE : (h + 1) * SIZE] = jnp.dot(probs, values, preferred_element_type=f32)


def row_kernel(at, s0, s2, s1, s3, before, total):
    refs = (s0, s1, s2, s3)
    x = at[0]
    place = [(x - k) & 3 for k in range(N_X)]
    last = [unpack(ref) for ref in refs]

    def between(k, end):
        return sum(jnp.where((place[m] > place[k]) & (place[m] < end), last[m], 0.0) for m in range(N_X))

    reach = [jnp.where(place[k] < x, jnp.exp(between(k, x)), 0.0) for k in range(N_X)]
    whole = [jnp.exp(between(k, N_X)) for k in range(N_X)]
    for h in range(HEADS):
        rows = slice(h * SIZE, (h + 1) * SIZE)
        states = [ref[rows, :].astype(f32) for ref in refs]
        before[rows, :] = sum(states[k] * reach[k][h : h + 1] for k in range(1, N_X))
        total[rows, :] = sum(states[k] * whole[k][h : h + 1] for k in range(N_X)).astype(bf16)
    pack(total, last[0] + last[1] + last[2] + last[3])
    lead = sum(jnp.where(place[k] < x, last[k], 0.0) for k in range(1, N_X))
    before[WIDE:, :] = jnp.concatenate([lead, lead], axis=0)


def normed_kernel(before, t2, t1, t3, a, b, c, d, g, inner, gain, out):
    lead = jnp.exp(before[WIDE : WIDE + HEADS, :])
    r1, r2 = unpack(t1), unpack(t2)
    reach2, reach3 = jnp.exp(r1), jnp.exp(r1 + r2)
    for h in range(HEADS):
        rows = slice(h * SIZE, (h + 1) * SIZE)
        one = slice(h, h + 1)
        earlier = (
            t1[rows, :].astype(f32) + t2[rows, :].astype(f32) * reach2[one] + t3[rows, :].astype(f32) * reach3[one]
        )
        carried = (earlier * lead[one] + before[rows, :]).astype(bf16)
        query = columns((a, b, c, d), h * SIZE).astype(f32)
        scaled = (query * jnp.exp(g[:, one])).astype(bf16)
        mixed = inner[:, rows] + jnp.dot(scaled, carried, preferred_element_type=f32)
        scale = lax.rsqrt(jnp.mean(mixed * mixed, axis=-1, keepdims=True) + norm_eps)
        out[:, rows] = (mixed * scale * gain[:, rows]).astype(bf16)


def whole_call(kernel, args, outs, name, flops, scalars=0):
    nbytes = sum(a.size * a.dtype.itemsize for a in args)
    return pl.pallas_call(
        kernel,
        out_shape=outs,
        in_specs=[pl.BlockSpec(memory_space=pltpu.SMEM)] * scalars
        + [pl.BlockSpec(memory_space=pltpu.VMEM)] * (len(args) - scalars),
        out_specs=jax.tree.map(lambda _: pl.BlockSpec(memory_space=pltpu.VMEM), outs),
        compiler_params=params(),
        cost_estimate=cost(flops, nbytes),
        name=name,
    )(*args)


def project_part(rows, w, outs, m):
    width = w.shape[2]
    part = jnp.dot(rows, w[m], preferred_element_type=f32).astype(bf16)
    for i, out in enumerate(outs):
        out[:, m * width : (m + 1) * width] = part[i * 64 : (i + 1) * 64]


def project_first_kernel(normed, w, own_low, sib_low, own_high, sib_high, held, sems):
    per = w.shape[0] // 4
    copies = [
        pltpu.make_async_copy(w.at[pl.ds(i * per, per)], held.at[pl.ds(i * per, per)], sems.at[i]) for i in range(4)
    ]
    for copy in copies:
        copy.start()
    far = normed[FAR : FAR + 128, :]
    for i in range(4):
        copies[i].wait()
        for m in range(i * per, (i + 1) * per):
            outs = (own_low, sib_low) if i < 2 else (own_high, sib_high)
            project_part(far, held.at[pl.ds(i // 2 * 2 * per, 2 * per)], outs, m - i // 2 * 2 * per)


def project_kernel(blocks, normed, w, *outs):
    rows = jnp.concatenate([normed[64 * b : 64 * b + 64, :] for b in blocks], axis=0)
    for m in range(w.shape[0]):
        project_part(rows, w, outs, m)


def project(normed, w, blocks):
    n_ctx, depth, width = w.shape
    vmem = pl.BlockSpec(memory_space=pltpu.VMEM)
    n = len(blocks)
    return pl.pallas_call(
        functools.partial(project_kernel, blocks),
        out_shape=[jax.ShapeDtypeStruct((64, n_ctx * width), bf16)] * n,
        in_specs=[vmem] * 2,
        out_specs=[vmem] * n,
        compiler_params=params(),
        cost_estimate=cost(2 * 64 * n * depth * n_ctx * width, 2 * depth * n_ctx * width),
        name="project",
    )(normed, w)


def gather_kernel(own, sib, up_plain, down_plain, out):
    mid = up_plain.shape[1]
    for start, other in ((0, down_plain), (mid, up_plain)):
        at = slice(start, start + mid)
        out[:, at] = own[:, at].astype(f32) + sib[:, at].astype(f32) + other[...].astype(f32)


def final_kernel(partial, up_sum, down_sum, out):
    mid = up_sum.shape[1]
    for start, other in ((0, up_sum), (mid, down_sum)):
        at = slice(start, start + mid)
        out[:, at] = (partial[:, at] + other[...].astype(f32)).astype(bf16)


def after(value, *others):
    return lax.optimization_barrier((value, *others))[0]


def plus(*terms):
    total = terms[0].astype(f32)
    for term in terms[1:]:
        total = total + term.astype(f32)
    return total.astype(bf16)


def body(activations, w_qkv, log_decay, gain, w_out):
    tp, ctx = lax.axis_index("tp"), lax.axis_index("ctx")
    y, core = tp // 2, tp % 2
    at = (ctx % N_X).astype(jnp.int32).reshape(1)
    w_all = lax.all_gather(w_out, "ctx", axis=0)

    cumul = jnp.cumsum(log_decay.T, axis=1)
    last = jnp.broadcast_to(cumul[:, -1:], (HEADS, SIZE))
    gt = jnp.roll(cumul.reshape(HEADS, N_Y, 2, 64), -y, axis=1)
    gt = jnp.where(core == 0, gt, gt[:, :, ::-1])
    gt = jnp.concatenate([gt[:, chip, half] for chip, half in PLACES], axis=1)
    g = gt.T
    chip, half = (jnp.array(np.repeat(np.array(p), 64), jnp.int32) for p in zip(*PLACES))
    pos = ((chip + y) & 3) * 128 + ((half + core) & 1) * 64 + jnp.arange(512, dtype=jnp.int32) % 64

    depth = activations.shape[1]
    mid = depth // 2
    low = activations[:, :mid]
    high = after(activations, low)[:, mid:]
    left_low, right_high = to_y(low, 1), to_y(high, -1)
    low_b, high_b = after((low, high), g, gt, last, at, pos)
    left_high, right_low = to_y(high_b, 1), to_y(low_b, -1)
    own2 = to_sibling(activations)
    own2 = after(own2, g, gt, last, at, pos)
    qkv_a, w_qkv = qkv([activations, own2], [(0, 0), (64, 0)], 128, w_qkv, True)
    left_low, right_high = after((left_low, right_high), qkv_a)
    far_low, far_high = to_y(left_low, 1), to_y(right_high, -1)
    low2, high2 = to_sibling(left_low), to_sibling(right_high)
    left_high2, right_low2 = to_sibling(left_high), to_sibling(right_low)
    halves = [(0, 0), (0, mid), (64, 0), (64, mid)]
    near = after((right_low, right_high, left_low, left_high), low2, high2)
    qkv_b = qkv(near, halves, 128, w_qkv)
    far_low, far_high = after((far_low, far_high), qkv_b)
    far_low2, far_high2 = to_sibling(far_low), to_sibling(far_high)
    near2 = after([right_low2, high2, low2, left_high2], far_low, far_high)
    qkv_c = qkv(near2, halves, 128, w_qkv)
    far_low2, far_high2 = after((far_low2, far_high2), qkv_c)
    qkv_d = qkv([far_low, far_high, far_low2, far_high2], halves, 128, w_qkv)
    rows = (qkv_b, qkv_a, qkv_c, qkv_d)

    packed = jax.ShapeDtypeStruct((WIDE + 16, SIZE), bf16)
    state = whole_call(state_kernel, (*rows, g, last), packed, "state", 2 * 512 * WIDE * SIZE)
    row = [state] + [to_x(state, k) for k in (2, 1, 3)]
    inner = whole_call(
        inner_kernel,
        (*rows, g, gt, pos.reshape(512, 1), pos.reshape(1, 512)),
        jax.ShapeDtypeStruct((512, WIDE), f32),
        "inner",
        4 * 512 * 512 * WIDE,
    )
    row = after(row, inner)
    before, total = whole_call(
        row_kernel, (at, *row), (jax.ShapeDtypeStruct((WIDE + 8, SIZE), f32), packed), "row", 10 * WIDE * SIZE, 1
    )
    totals = [to_z(total, k) for k in (2, 1, 3)]
    normed = whole_call(
        normed_kernel,
        (before, *totals, *rows, g, inner, gain.reshape(1, WIDE)),
        jax.ShapeDtypeStruct((512, WIDE), bf16),
        "normed",
        2 * 512 * WIDE * SIZE,
    )
    vmem = pl.BlockSpec(memory_space=pltpu.VMEM)
    half = jax.ShapeDtypeStruct((64, mid), bf16)
    own_low, sib_low, own_high, sib_high, w = pl.pallas_call(
        project_first_kernel,
        out_shape=[half] * 4 + [pltpu.VMEM(w_all.shape, bf16)],
        in_specs=[vmem, pl.BlockSpec(memory_space=pltpu.HBM)],
        out_specs=[vmem] * 5,
        scratch_shapes=[pltpu.SemaphoreType.DMA((4,))],
        compiler_params=params(),
        cost_estimate=cost(256 * w_all.size, 2 * w_all.size),
        name="project",
    )(normed, pltpu.with_memory_space_constraint(w_all, pltpu.HBM))

    sib_low, sib_high = to_sibling(sib_low), to_sibling(sib_high)
    near_parts = project(normed, w, (0, 4, 1, 5))
    sib_low, sib_high = after((sib_low, sib_high), near_parts)
    far = plus(own_low, sib_low), plus(own_high, sib_high)
    from_l, from_r = to_y(far[0], 1), to_y(far[1], -1)
    up_own, up_sib, down_own, down_sib = after(near_parts, *far)
    up_sib, down_sib = to_sibling(up_sib), to_sibling(down_sib)
    up_plain = plus(up_own[:, mid:], up_sib[:, mid:])
    down_plain = plus(down_own[:, :mid], down_sib[:, :mid])
    normed = after(normed, up_plain, down_plain)
    up_plain, down_plain = to_y(up_plain, 1), to_y(down_plain, -1)
    here_own, here_sib = project(normed, w, (2, 3))
    from_l, from_r = after((from_l, from_r), here_own)
    up_sum = to_y(plus(up_own[:, :mid], up_sib[:, :mid], from_l), 1)
    down_sum = to_y(plus(down_own[:, mid:], down_sib[:, mid:], from_r), -1)
    here_sib = to_sibling(here_sib)
    partial = whole_call(
        gather_kernel,
        (here_own, here_sib, up_plain, down_plain),
        jax.ShapeDtypeStruct((64, depth), f32),
        "gather",
        3 * 64 * depth,
    )
    up_sum, down_sum = after((up_sum, down_sum), partial)
    return whole_call(
        final_kernel, (partial, up_sum, down_sum), jax.ShapeDtypeStruct((64, depth), bf16), "final", 64 * depth
    )


def solution(mesh):
    in_specs = (
        P(("ctx", "tp"), None),
        P(None, None, "tp"),
        P("ctx", "tp"),
        P("tp"),
        P("tp", "ctx"),
    )
    out_specs = P(("ctx", "tp"), None)
    return jax.shard_map(body, mesh=mesh, in_specs=in_specs, out_specs=out_specs, check_vma=False)
```
